256 devices in a mesh: space: 16 (over z, y_lo), replica: 16 (over x, y_hi, core).
Axes of the slice: x: 4, y: 4 (y_hi: 2, y_lo: 2; y = y_hi * 2 + y_lo), z: 8, core: 2. Of those that a mesh axis runs over, the one named last changes fastest.
Arguments:
- hologram: bfloat16 [16, 32, 64, 64, 128], P('replica', 'space'), may hold values from -6 to 6
- weight: bfloat16 [3, 3, 128, 128], replicated, may hold values from -0.1875 to 0.1875
- conv_bias: float32 [128], replicated, may hold values from -3 to 3
- cotangent: bfloat16 [16, 32, 64, 64, 128], P('replica', 'space'), may hold values from -6 to 6
- tissue: int32 [16, 32, 4096], P('replica', 'space'), may hold values 0 or 1
- owners: int32 [16, 32], P('replica'), may hold values from 0 to 31, each once within a row
- neighbours: int32 [16, 8, 32], P('replica'), may hold values from -1 to 31, as said below
Outputs:
- features: bfloat16 [16, 32, 64, 64, 128], P('replica', 'space')
- input_grad: bfloat16 [16, 32, 64, 64, 128], P('replica', 'space')
- weight_grad: float32 [3, 3, 128, 128], replicated
- bias_grad: float32 [128], replicated
The draws below stay inside these ranges and needn't reach their ends.
Inputs may be any that keep to these rules, and one draw needn't show every extreme that they name: `owners`: each row is a permutation of the tiles; slot j lies on index j // 2 of space. `neighbours`: the tiles of a hologram stand on a grid of 64 positions, 8 to a row; entry [s, k, t] is the tile at the position next to tile t in direction k (north, south, west, east, north-west, north-east, south-west, south-east), or -1 where that position lies outside the grid or holds no tissue tile. The relation is symmetric.
All inputs are finite; a program needn't handle non-finite values. No bound on the sum of `tissue` on one device may be relied on, other than what follows from the above.
Results may differ from the reference program's by a relative error of at most 0.0075.
Values may be sent and summed in bfloat16 or wider, within the bound.
A program may use at most 64 MiB of HBM per device.

```python
import math
import jax
import jax.numpy as jnp
from jax import lax

C = 128
TILE = 64
GRID_COLS = 8
SLOTS = 32
POSITIONS = 64
SAMPLES = 16


def grid_layout(key):
    picked = jax.random.permutation(key, POSITIONS - 2)[:SLOTS - 2].astype(jnp.int32)
    ends = jnp.array([POSITIONS - 2, POSITIONS - 1], dtype=jnp.int32)
    chosen = jnp.sort(jnp.concatenate([picked, ends]))
    pos_tile = jnp.full((POSITIONS,), -1, jnp.int32).at[chosen].set(jnp.arange(SLOTS, dtype=jnp.int32))
    grid_rows = POSITIONS // GRID_COLS
    row_at = chosen // GRID_COLS
    col_at = chosen % GRID_COLS
    steps_list = [(-1, 0), (1, 0), (0, -1), (0, 1), (-1, -1), (-1, 1), (1, -1), (1, 1)]
    found = []
    for step_pair in steps_list:
        row_new = row_at + step_pair[0]
        col_new = col_at + step_pair[1]
        inside = (row_new >= 0) & (row_new < grid_rows) & (col_new >= 0) & (col_new < GRID_COLS)
        index = jnp.clip(row_new, 0, grid_rows - 1) * GRID_COLS + jnp.clip(col_new, 0, GRID_COLS - 1)
        found.append(jnp.where(inside, pos_tile[index], -1))
    return jnp.stack(found).astype(jnp.int32)


def draw_neighbours(key, part):
    key = jax.random.fold_in(key, 7)
    sample_keys = jax.random.split(key, SAMPLES)
    return jax.vmap(grid_layout)(sample_keys)


def touch_ends(drawn, stream_key, smallest, high):
    index_at = [jax.random.randint(jax.random.fold_in(stream_key, axis), (), 0, length) for axis, length in enumerate(drawn.shape)]
    longest = drawn.shape.index(max(drawn.shape))
    beside = index_at[:longest] + [(index_at[longest] + 1) % drawn.shape[longest]] + index_at[longest + 1:]
    return drawn.at[tuple(index_at)].set(smallest).at[tuple(beside)].set(high)


def levels(rng, extent, pieces, low, largest):
    factor_of, own = 1.0, jax.random.fold_in(rng, 6)
    for position, parts in pieces:
        draws = jnp.exp(jax.random.uniform(jax.random.fold_in(own, position), (parts,), jnp.float32, low / len(pieces), largest / len(pieces)))
        factor_of = factor_of * jnp.repeat(draws, extent[position] // parts).reshape([-1 if axis == position else 1 for axis in range(len(extent))])
    return factor_of


def normal_values(stream_key, extent, scale, limit, shards=(), kind=jnp.bfloat16):
    gain = levels(stream_key, extent, shards, -0.22, 0.18) if shards else 1.0
    drawn = jax.random.normal(stream_key, extent, jnp.float32) * scale * gain
    return jnp.minimum(jnp.maximum(drawn, -limit), limit).astype(kind)


def setup_inputs(seed: int = 0) -> dict:
    arg_keys = jax.random.split(jax.random.key(seed), 8)
    return {
        "hologram": normal_values(arg_keys[0], (SAMPLES, SLOTS, TILE, TILE, C), 1.0, 6.0, ((0, 16), (1, 16))),
        "weight": normal_values(arg_keys[1], (3, 3, C, C), (9 * C) ** -0.5, 0.1875),
        "conv_bias": normal_values(arg_keys[2], (C,), 0.5, 3.0, (), jnp.float32),
        "cotangent": normal_values(arg_keys[3], (SAMPLES, SLOTS, TILE, TILE, C), 1.0, 6.0, ((0, 16), (1, 16))),
        "tissue": touch_ends((jax.random.randint(arg_keys[4], (SAMPLES, SLOTS, TILE * TILE), 0, 4) < 3).astype(jnp.int32), jax.random.fold_in(arg_keys[4], 1), 0, 1),
        "owners": jax.vmap(lambda own: jax.random.permutation(own, SLOTS))(jax.random.split(arg_keys[5], SAMPLES)).reshape((SAMPLES, SLOTS)).astype(jnp.int32),
        "neighbours": draw_neighbours(jax.random.fold_in(arg_keys[7], 71), 0),
    }


def edge_pair(tiles):
    rows = jnp.stack([tiles[:, 0], tiles[:, -1]], axis=1)
    cols = jnp.stack([tiles[:, :, 0], tiles[:, :, -1]], axis=1)
    return (rows, cols)

def neighbour_slots(owners_row, neighbours_row, my_slots):
    count = owners_row.shape[0]
    positions = jnp.arange(count, dtype=jnp.int32)
    my_tiles = lax.optimization_barrier(jnp.sum(jnp.where(positions[None, :] == my_slots[:, None], owners_row[None, :], 0), axis=1))
    near = lax.optimization_barrier(jnp.sum(jnp.where(positions[None, None, :] == my_tiles[None, :, None], neighbours_row[:, None, :], 0), axis=2))
    slot_of = lax.optimization_barrier(jnp.sum(jnp.where(owners_row[None, None, :] == near[:, :, None], positions[None, None, :], 0), axis=2))
    return (slot_of.astype(jnp.int32), near >= 0)

def assemble(tiles, rows_all, cols_all, slot_of, present):

    def face(table, direction, side):
        got = table[slot_of[direction], side]
        return jnp.where(present[direction][:, None, None], got, jnp.zeros_like(got))

    def corner(direction, side, end):
        got = rows_all[slot_of[direction], side, end]
        return jnp.where(present[direction][:, None], got, jnp.zeros_like(got))
    north = face(rows_all, 0, 1)
    south = face(rows_all, 1, 0)
    west = face(cols_all, 2, 1)
    east = face(cols_all, 3, 0)
    top = jnp.concatenate([corner(4, 1, -1)[:, None], north, corner(5, 1, 0)[:, None]], axis=1)
    bottom = jnp.concatenate([corner(6, 0, -1)[:, None], south, corner(7, 0, 0)[:, None]], axis=1)
    middle = jnp.concatenate([west[:, :, None], tiles, east[:, :, None]], axis=2)
    return jnp.concatenate([top[:, None], middle, bottom[:, None]], axis=1)

def sample_layer(tiles, weight, conv_bias, cot_tiles, tissue_rows, owners_row, neighbours_row):
    count, height, width, chan = tiles.shape
    my_slots = jnp.arange(count, dtype=jnp.int32)
    slot_of, present = neighbour_slots(owners_row, neighbours_row, my_slots)
    rows, cols = edge_pair(tiles)
    padded = assemble(tiles, rows, cols, slot_of, present)
    pre = jnp.zeros((count * height * width, chan), jnp.float32)
    for row_off in range(3):
        for col_off in range(3):
            window = padded[:, row_off:row_off + height, col_off:col_off + width].reshape(-1, chan)
            pre = pre + jnp.dot(window, weight[row_off, col_off], preferred_element_type=jnp.float32)
    pre = pre.reshape(count, height, width, chan) + conv_bias
    keep = tissue_rows.reshape(count, height, width, 1).astype(jnp.float32)
    sigma = jax.nn.sigmoid(pre)
    features = (pre * sigma * keep).astype(jnp.bfloat16)
    slope = sigma * (1.0 + pre * (1.0 - sigma))
    grad_pre = (cot_tiles.astype(jnp.float32) * keep * slope).astype(jnp.bfloat16)
    grad_rows, grad_cols = edge_pair(grad_pre)
    grad_padded = assemble(grad_pre, grad_rows, grad_cols, slot_of, present)
    flat_grad = grad_pre.reshape(-1, chan)
    input_grad = jnp.zeros((count * height * width, chan), jnp.float32)
    weight_rows = []
    for row_off in range(3):
        weight_cols = []
        for col_off in range(3):
            window = grad_padded[:, 2 - row_off:2 - row_off + height, 2 - col_off:2 - col_off + width].reshape(-1, chan)
            input_grad = input_grad + lax.dot_general(window, weight[row_off, col_off], (((1,), (1,)), ((), ())), preferred_element_type=jnp.float32)
            source = padded[:, row_off:row_off + height, col_off:col_off + width].reshape(-1, chan)
            weight_cols.append(lax.dot_general(source, flat_grad, (((0,), (0,)), ((), ())), preferred_element_type=jnp.float32))
        weight_rows.append(jnp.stack(weight_cols))
    local_w = jnp.stack(weight_rows)
    local_b = lax.optimization_barrier(jnp.sum(flat_grad.astype(jnp.float32), axis=0))
    input_grad = input_grad.reshape(count, height, width, chan).astype(jnp.bfloat16)
    return (features, input_grad, local_w, local_b)

def reference(hologram, weight, conv_bias, cotangent, tissue, owners, neighbours):

    def one_sample(items):
        tiles, cot_tiles, tissue_rows, owners_row, neighbours_row = items
        return sample_layer(tiles, weight, conv_bias, cot_tiles, tissue_rows, owners_row, neighbours_row)
    features, input_grad, local_w, local_b = lax.map(one_sample, (hologram, cotangent, tissue, owners, neighbours))
    scale = 1.0 / math.sqrt(SAMPLES * SLOTS * TILE * TILE)
    weight_grad = lax.optimization_barrier(jnp.sum(local_w, axis=0)) * scale
    bias_grad = lax.optimization_barrier(jnp.sum(local_b, axis=0)) * scale
    return (features, input_grad, weight_grad, bias_grad)
```

```python
import functools

import jax
import jax.numpy as jnp
from jax import lax
from jax.experimental import pallas as pl
from jax.experimental.pallas import tpu as pltpu
from jax.sharding import PartitionSpec as P

MESH = pl.DeviceIdType.MESH
BF = jnp.bfloat16
F32 = jnp.float32

NS = 16
NR = 16
NZ = 8
NP = 16
T = 2
H = 64
C = 128
PITCH = 80
WEST, FIRST, EAST = 7, 8, 72
HALF = 640
CH = HALF // NP
OFF = float(2**20)
PB = 4
DIRS = 4


def at80(row, off):
    return pl.multiple_of(row * PITCH, 8) + off


def kernel(
    holo, weight, bias, cot, tissue, owners, owners_s, neigh,
    feat, ingrad, wgrad, bgrad,
    hv, cv, fv, gv, iv, frame, x3, g3, w4, w4g, acc, bacc, drops, cfr, slots_v, slots_s,
    s1, r1, s2, r2, arb, arcv, half, brcv, csrc, crcv, dsrc, dall, erc,
    lsem, osem, ss1, rs1, ss2, rs2, sa, ra, sb, rb, sc, rc, sd, rd, se, re,
):
    sp = lax.axis_index("space")
    rp = lax.axis_index("replica")
    z, ylo = lax.div(sp, 2), lax.rem(sp, 2)
    core = lax.rem(rp, 2)
    plane = lax.div(rp, 4) * 4 + lax.rem(lax.div(rp, 2), 2) * 2 + ylo

    def plane_dev(p):
        return (z * 2 + lax.rem(p, 2), lax.div(p, 2) * 2 + core)

    def z_dev(k):
        return (k * 2 + ylo, rp)

    partner = (sp, rp + 1 - 2 * core)

    def load_h(t):
        return pltpu.make_async_copy(holo.at[t], hv.at[t], lsem.at[t])

    def load_c(t):
        return pltpu.make_async_copy(cot.at[t], cv.at[t], lsem.at[T + t])

    for t in range(T):
        load_h(t).start()
    for t in range(T):
        load_c(t).start()

    barrier = pltpu.get_barrier_semaphore()

    def greet(o, carry):
        pl.semaphore_signal(
            barrier, inc=1, device_id=(lax.rem(sp + o, NS), rp), device_id_type=MESH
        )
        pl.semaphore_signal(
            barrier, inc=1, device_id=plane_dev(lax.rem(plane + o, NP)), device_id_type=MESH
        )
        return carry

    lax.fori_loop(1, NS, greet, 0)
    pl.semaphore_signal(barrier, inc=1, device_id=partner, device_id_type=MESH)

    def copy1(ph, m, src):
        return pltpu.make_async_remote_copy(
            src_ref=s1.at[ph, m], dst_ref=r1.at[ph, src],
            send_sem=ss1.at[ph, m], recv_sem=rs1.at[ph, src],
            device_id=(m, rp), device_id_type=MESH,
        )

    def copy2(ph, j, src):
        return pltpu.make_async_remote_copy(
            src_ref=s2.at[ph, j], dst_ref=r2.at[ph, src],
            send_sem=ss2.at[ph, j], recv_sem=rs2.at[ph, src],
            device_id=(j, rp), device_id_type=MESH,
        )

    def over_space(fn):
        def step(o, carry):
            fn(lax.rem(sp + o, NS))
            return carry

        lax.fori_loop(1, NS, step, 0)

    def exchange_out(ph, tiles):
        for t in range(T):
            top = tiles[t, 0]
            bottom = tiles[t, H - 1]
            left = frame[t, pl.ds(PITCH + FIRST, H, stride=PITCH), :].astype(BF)
            right = frame[t, pl.ds(PITCH + FIRST + H - 1, H, stride=PITCH), :].astype(BF)
            for d, line in enumerate((bottom, top, right, left)):
                for q in range(4):
                    s1[ph, 4 * d + q, t] = line[16 * q : 16 * q + 16]
            for k, (y, x) in enumerate(((H - 1, H - 1), (H - 1, 0), (0, H - 1), (0, 0))):
                cfr[NS, pl.ds(t * 4 + k, 1), :] = frame[
                    t, pl.ds((y + 1) * PITCH + FIRST + x, 1), :
                ]
        block = cfr[NS].astype(BF)
        for m in range(NS):
            s1[ph, m, T] = block
        r1[ph, sp] = s1[ph, sp]

    def exchange_send1(ph):
        over_space(lambda m: copy1(ph, m, sp).start())

    def exchange_route(ph):
        over_space(lambda i: copy1(ph, i, i).wait_recv())
        mine = lax.div(sp, 4)

        def route(j, carry):
            for u in range(T):
                s = slots_s[mine, T * j + u]
                s2[ph, j, u] = r1[ph, lax.div(s, 2), lax.rem(s, 2)]
            return carry

        lax.fori_loop(0, NS, route, 0)
        over_space(lambda j: copy2(ph, j, sp).start())
        r2[ph, sp] = s2[ph, sp]

    def exchange_in(ph):
        cfr[NS] = jnp.zeros((16, C), F32)

        def widen(i, carry):
            cfr[i] = r1[ph, i, T].astype(F32)
            return carry

        lax.fori_loop(0, NS, widen, 0)
        over_space(lambda i: copy2(ph, i, i).wait_recv())
        for t in range(T):
            for k, (row, col) in enumerate(
                ((0, WEST), (0, EAST), (H + 1, WEST), (H + 1, EAST))
            ):
                s = slots_s[DIRS + k, T * sp + t]
                frame[t, pl.ds(row * PITCH + col, 1), :] = cfr[
                    lax.div(s, 2), pl.ds(lax.rem(s, 2) * 4 + k, 1), :
                ]
            for q in range(4):
                frame[t, pl.ds(FIRST + 16 * q, 16), :] = r2[ph, q, t].astype(F32)
                frame[t, pl.ds((H + 1) * PITCH + FIRST + 16 * q, 16), :] = r2[
                    ph, 4 + q, t
                ].astype(F32)
                for d, col in ((2, WEST), (3, EAST)):
                    frame[t, pl.ds((16 * q + 1) * PITCH + col, 16, stride=PITCH), :] = r2[
                        ph, 4 * d + q, t
                    ].astype(F32)

    def exchange_end(ph):
        over_space(lambda m: copy1(ph, m, sp).wait_send())
        over_space(lambda m: copy2(ph, m, sp).wait_send())

    for t in range(T):
        load_h(t).wait()

        def fill(y, carry):
            frame[t, pl.ds(at80(y + 1, FIRST), H), :] = hv[t, y].astype(F32)
            return carry

        lax.fori_loop(0, H, fill, 0)
    cfr[NS] = jnp.zeros((16, C), F32)
    exchange_out(0, hv)
    pl.semaphore_wait(barrier, 2 * (NS - 1) + 1)
    exchange_send1(0)

    own = jnp.broadcast_to(owners[...], (2 * DIRS, 2 * NS))
    near = jnp.full((2 * DIRS, 2 * NS), -1, jnp.int32)
    for tile in range(2 * NS):
        near = jnp.where(own == tile, neigh[:, tile : tile + 1], near)
    found = jnp.full((2 * DIRS, 2 * NS), 2 * NS, jnp.int32)
    for slot in range(2 * NS):
        found = jnp.where(near == owners_s[0, slot], slot, found)
    slots_v[:, 0 : 2 * NS] = found
    to_smem = pltpu.make_async_copy(slots_v, slots_s, lsem.at[2 * T])
    to_smem.start()

    zeros = jnp.zeros((C, C), BF)
    for r in range(4):
        for b in range(3):
            for q in range(2):
                a = r - q
                rows, cols = pl.ds((r * 3 + b) * C, C), pl.ds(q * C, C)
                if 0 <= a <= 2:
                    w4[rows, cols] = weight[a, b]
                    w4g[rows, cols] = weight[2 - a, 2 - b].astype(F32).T.astype(BF)
                else:
                    w4[rows, cols] = zeros
                    w4g[rows, cols] = zeros
    line = lax.broadcasted_iota(jnp.int32, (C, 2 * C), 0)
    lane = lax.broadcasted_iota(jnp.int32, (C, 2 * C), 1)
    w4[12 * C : 13 * C, :] = jnp.where((line < H) == (lane < C), -OFF, 0.0).astype(BF)
    bacc[...] = jnp.zeros_like(bacc)
    acc[...] = jnp.zeros_like(acc)
    for t in range(T):
        for p in range(H // 2):
            drops[t * (H // 2) + p : t * (H // 2) + p + 1, :] = (
                1 - tissue[t : t + 1, p * C : (p + 1) * C]
            ).astype(F32)
    for i in range(2):
        r1[i, NS] = jnp.zeros((3, 16, C), BF)
    to_smem.wait()

    exchange_route(0)
    exchange_in(0)

    def shifts(dst):
        for t in range(T):

            def step(y, carry):
                for b in range(3):
                    dst[t, y, :, b * C : (b + 1) * C] = frame[
                        t, pl.ds(at80(y, WEST + b), H), :
                    ].astype(BF)
                return carry

            lax.fori_loop(0, H + 2, step, 0)

    shifts(x3)
    for t in range(T):
        load_c(t).wait()

    nb = (H // 2) // PB
    bias2 = jnp.concatenate([bias[...], bias[...]], axis=1)
    eye = (
        lax.broadcasted_iota(jnp.int32, (H, C), 0)
        == lax.broadcasted_iota(jnp.int32, (H, C), 1) % H
    )

    def window(src, t, p):
        return jnp.concatenate([src[t, 2 * p + r] for r in range(4)], axis=1)

    def forward(i, carry):
        t, p0 = lax.div(i, nb), lax.rem(i, nb) * PB
        parts = []
        for k in range(PB):
            drop = jnp.where(eye, drops[pl.ds(t * (H // 2) + p0 + k, 1), :], 0.0).astype(BF)
            parts.append(jnp.concatenate([window(x3, t, p0 + k), drop], axis=1))
        pre = jnp.dot(
            jnp.concatenate(parts, axis=0), w4[...], preferred_element_type=F32
        ) + bias2
        sigma = 0.5 * jnp.tanh(0.5 * pre) + 0.5
        act = pre * sigma
        slope = sigma + act * (1.0 - sigma)
        total = jnp.zeros((8, C), F32)
        for k in range(PB):
            for q in range(2):
                y = 2 * (p0 + k) + q
                rows, cols = slice(k * H, (k + 1) * H), slice(q * C, (q + 1) * C)
                fv[t, y] = act[rows, cols].astype(BF)
                g = (cv[t, y].astype(F32) * slope[rows, cols]).astype(BF)
                gv[t, y] = g
                wide = g.astype(F32)
                frame[t, pl.ds(at80(y + 1, FIRST), H), :] = wide
                total = total + jnp.sum(wide.reshape(H // 8, 8, C), axis=0)
        bacc[...] += total
        return carry

    lax.fori_loop(0, T * nb, forward, 0)
    out_f = pltpu.make_async_copy(fv, feat, osem.at[0])
    out_f.start()

    exchange_out(1, gv)
    exchange_send1(1)

    WB = 8

    def weights(t):
        def step(i, carry):
            p0 = i * WB
            left = jnp.concatenate(
                [
                    jnp.concatenate(
                        [gv[t, 2 * (p0 + k) + q] for k in range(WB)], axis=0
                    ).astype(F32).T.astype(BF)
                    for q in range(2)
                ],
                axis=0,
            )
            right = jnp.concatenate([window(x3, t, p0 + k) for k in range(WB)], axis=0)
            acc[...] += jnp.dot(left, right, preferred_element_type=F32)
            return carry

        lax.fori_loop(0, (H // 2) // WB, step, 0)

    weights(0)
    exchange_route(1)
    weights(1)

    for tap in range(9):
        a, b = tap // 3, tap % 3
        lo = slice((a * 3 + b) * C, (a * 3 + b + 1) * C)
        hi = slice(((a + 1) * 3 + b) * C, ((a + 1) * 3 + b + 1) * C)
        block = (acc[0:C, lo] + acc[C : 2 * C, hi]).T
        if tap < 4:
            arb[0, tap * C : (tap + 1) * C] = block
        elif tap == 4:
            arb[0, 4 * C : 4 * C + H] = block[:H]
            arb[1, 0:H] = block[H:]
        else:
            arb[1, H + (tap - 5) * C : H + (tap - 4) * C] = block
    bsum = jnp.sum(bacc[...], axis=0, keepdims=True)
    first = lax.broadcasted_iota(jnp.int32, (HALF - 576, C), 0) == 0
    for i in range(2):
        arb[i, 576:HALF] = jnp.where(first, bsum, 0.0)

    copy_a = pltpu.make_async_remote_copy(
        src_ref=arb.at[1 - core], dst_ref=arcv, send_sem=sa, recv_sem=ra,
        device_id=partner, device_id_type=MESH,
    )
    copy_a.start()

    def chunk(p):
        return pl.ds(pl.multiple_of(p * CH, 8), CH)

    def copy_b(p, src):
        return pltpu.make_async_remote_copy(
            src_ref=half.at[chunk(p)], dst_ref=brcv.at[src],
            send_sem=sb.at[p], recv_sem=rb.at[src],
            device_id=plane_dev(p), device_id_type=MESH,
        )

    def copy_c(k, src):
        return pltpu.make_async_remote_copy(
            src_ref=csrc, dst_ref=crcv.at[src], send_sem=sc.at[k], recv_sem=rc.at[src],
            device_id=z_dev(k), device_id_type=MESH,
        )

    def copy_d(p, src):
        return pltpu.make_async_remote_copy(
            src_ref=dsrc, dst_ref=dall.at[chunk(src)], send_sem=sd.at[p], recv_sem=rd.at[src],
            device_id=plane_dev(p), device_id_type=MESH,
        )

    copy_e = pltpu.make_async_remote_copy(
        src_ref=dall, dst_ref=erc, send_sem=se, recv_sem=re,
        device_id=partner, device_id_type=MESH,
    )

    def over_plane(fn):
        def step(o, carry):
            fn(lax.rem(plane + o, NP))
            return carry

        lax.fori_loop(1, NP, step, 0)

    def over_z(fn):
        def step(o, carry):
            fn(lax.rem(z + o, NZ))
            return carry

        lax.fori_loop(1, NZ, step, 0)

    def stage_b():
        copy_a.wait_recv()
        half[...] = arb[core] + arcv[...]
        over_plane(lambda p: copy_b(p, plane).start())
        brcv[plane] = half[chunk(plane)]

    def stage_c():
        over_plane(lambda p: copy_b(p, p).wait_recv())
        total = brcv[0]
        for p in range(1, NP):
            total = total + brcv[p]
        csrc[...] = total
        over_z(lambda k: copy_c(k, z).start())
        crcv[z] = total

    def stage_d():
        over_z(lambda k: copy_c(k, k).wait_recv())
        total = crcv[0]
        for k in range(1, NZ):
            total = total + crcv[k]
        total = total * float(NS * NR * T * H * H) ** -0.5
        dsrc[...] = total
        over_plane(lambda p: copy_d(p, plane).start())
        dall[chunk(plane)] = total

    def stage_e():
        over_plane(lambda p: copy_d(p, p).wait_recv())
        copy_e.start()

    exchange_in(1)
    stage_b()
    shifts(g3)

    def backward(t):
        def step(i, carry):
            p0 = i * PB
            got = jnp.dot(
                jnp.concatenate([window(g3, t, p0 + k) for k in range(PB)], axis=0),
                w4g[...],
                preferred_element_type=F32,
            )
            for k in range(PB):
                for q in range(2):
                    iv[t, 2 * (p0 + k) + q] = got[
                        k * H : (k + 1) * H, q * C : (q + 1) * C
                    ].astype(BF)
            return carry

        lax.fori_loop(0, nb, step, 0)
        pltpu.make_async_copy(iv.at[t], ingrad.at[t], osem.at[1 + t]).start()

    stage_c()
    backward(0)
    stage_d()
    backward(1)
    stage_e()

    exchange_end(0)
    exchange_end(1)
    copy_a.wait_send()
    over_plane(lambda p: copy_b(p, plane).wait_send())
    over_z(lambda k: copy_c(k, z).wait_send())
    over_plane(lambda p: copy_d(p, plane).wait_send())
    out_f.wait()
    for t in range(T):
        pltpu.make_async_copy(iv.at[t], ingrad.at[t], osem.at[1 + t]).wait()
    copy_e.wait()
    rows_mine = pl.ds(pl.multiple_of(core * 576, 8), 576)
    rows_other = pl.ds(pl.multiple_of((1 - core) * 576, 8), 576)
    wgrad[rows_mine, :] = dall[0:576]
    wgrad[rows_other, :] = erc[0:576]
    bgrad[...] = dall[576:577]


def local(hologram, weight, conv_bias, cotangent, tissue, owners, neighbours):
    vmem = pl.BlockSpec(memory_space=pltpu.VMEM)
    smem = pl.BlockSpec(memory_space=pltpu.SMEM)
    hbm = pl.BlockSpec(memory_space=pl.ANY)
    tiles = jax.ShapeDtypeStruct((T, H, H, C), BF)
    dma = pltpu.SemaphoreType.DMA
    feat, ingrad, wgrad, bgrad = pl.pallas_call(
        kernel,
        out_shape=(
            tiles,
            tiles,
            jax.ShapeDtypeStruct((9 * C, C), F32),
            jax.ShapeDtypeStruct((1, C), F32),
        ),
        in_specs=[hbm, vmem, vmem, hbm, vmem, vmem, smem, vmem],
        out_specs=(hbm, hbm, vmem, vmem),
        scratch_shapes=[
            pltpu.VMEM((T, H, H, C), BF),
            pltpu.VMEM((T, H, H, C), BF),
            pltpu.VMEM((T, H, H, C), BF),
            pltpu.VMEM((T, H, H, C), BF),
            pltpu.VMEM((T, H, H, C), BF),
            pltpu.VMEM((T, (H + 2) * PITCH, C), F32),
            pltpu.VMEM((T, H + 2, H, 3 * C), BF),
            pltpu.VMEM((T, H + 2, H, 3 * C), BF),
            pltpu.VMEM((13 * C, 2 * C), BF),
            pltpu.VMEM((12 * C, 2 * C), BF),
            pltpu.VMEM((2 * C, 12 * C), F32),
            pltpu.VMEM((8, C), F32),
            pltpu.VMEM((T * H // 2, C), F32),
            pltpu.VMEM((NS + 1, 16, C), F32),
            pltpu.VMEM((8, C), jnp.int32),
            pltpu.SMEM((8, C), jnp.int32),
            pltpu.VMEM((2, NS, 3, 16, C), BF),
            pltpu.VMEM((2, NS + 1, 3, 16, C), BF),
            pltpu.VMEM((2, NS, T, 16, C), BF),
            pltpu.VMEM((2, NS, T, 16, C), BF),
            pltpu.VMEM((2, HALF, C), F32),
            pltpu.VMEM((HALF, C), F32),
            pltpu.VMEM((HALF, C), F32),
            pltpu.VMEM((NP, CH, C), F32),
            pltpu.VMEM((CH, C), F32),
            pltpu.VMEM((NZ, CH, C), F32),
            pltpu.VMEM((CH, C), F32),
            pltpu.VMEM((HALF, C), F32),
            pltpu.VMEM((HALF, C), F32),
            dma((2 * T + 1,)),
            dma((1 + T,)),
            dma((2, NS)), dma((2, NS)), dma((2, NS)), dma((2, NS)),
            dma, dma,
            dma((NP,)), dma((NP,)),
            dma((NZ,)), dma((NZ,)),
            dma((NP,)), dma((NP,)),
            dma, dma,
        ],
        compiler_params=pltpu.CompilerParams(
            collective_id=0, has_side_effects=True, vmem_limit_bytes=56 * 2**20
        ),
        cost_estimate=pl.CostEstimate(
            flops=7247757312, bytes_accessed=10 * 2**20, transcendentals=2**20
        ),
        name="unet_conv_step",
    )(
        hologram[0], weight, conv_bias[None], cotangent[0], tissue[0], owners, owners,
        neighbours[0],
    )
    return (
        feat[None], ingrad[None], wgrad.reshape(3, 3, C, C), bgrad.reshape(C)
    )


def solution(mesh):
    return jax.shard_map(
        local,
        mesh=mesh,
        in_specs=(
            P("replica", "space", None, None, None),
            P(),
            P(),
            P("replica", "space", None, None, None),
            P("replica", "space", None),
            P("replica", None),
            P("replica", None, None),
        ),
        out_specs=(
            P("replica", "space", None, None, None),
            P("replica", "space", None, None, None),
            P(),
            P(),
        ),
        check_vma=False,
    )
```

```python
import functools

import jax
import jax.numpy as jnp
from jax import lax
from jax.experimental import pallas as pl
from jax.experimental.pallas import tpu as pltpu
from jax.sharding import PartitionSpec as P

MESH = pl.DeviceIdType.MESH
BF = jnp.bfloat16
F32 = jnp.float32

NS = 16
NR = 16
NZ = 8
NP = 16
T = 2
H = 64
C = 128
PITCH = 80
WEST, FIRST, EAST = 7, 8, 72
HALF = 640
CH = HALF // NP
OFF = float(2**20)
PB = 16
WB = 32
DIRS = 4


def at80(row, off):
    return pl.multiple_of(row * PITCH, 8) + off


def kernel(
    holo, weight, bias, cot, tissue, owners, owners_s, neigh,
    feat, ingrad, packed,
    hv, cv, fv, gv, iv, fh, fg, x3, g3, w4, w4g, w9, w9g, pb, acc, bacc, raw2, drops,
    cotb, fb, gb, cfr, slots_v, slots_s,
    s1, r1, s2, r2, arb, arcv, half, brcv, csrc, crcv, dsrc, dall, erc,
    lsem, osem, ss1, rs1, ss2, rs2, sa, ra, sb, rb, sc, rc, sd, rd, se, re,
):
    sp = lax.axis_index("space")
    rp = lax.axis_index("replica")
    z, ylo = lax.div(sp, 2), lax.rem(sp, 2)
    core = lax.rem(rp, 2)
    plane = lax.div(rp, 4) * 4 + lax.rem(lax.div(rp, 2), 2) * 2 + ylo

    def plane_dev(p):
        return (z * 2 + lax.rem(p, 2), lax.div(p, 2) * 2 + core)

    def z_dev(k):
        return (k * 2 + ylo, rp)

    partner = (sp, rp + 1 - 2 * core)

    def load_h(t):
        return pltpu.make_async_copy(holo.at[t], hv.at[t], lsem.at[t])

    def load_c(t):
        return pltpu.make_async_copy(cot.at[t], cv.at[t], lsem.at[T + t])

    for t in range(T):
        load_h(t).start()
    for t in range(T):
        load_c(t).start()

    barrier = pltpu.get_barrier_semaphore()

    def greet(o, carry):
        pl.semaphore_signal(
            barrier, inc=1, device_id=(lax.rem(sp + o, NS), rp), device_id_type=MESH
        )
        pl.semaphore_signal(
            barrier, inc=1, device_id=plane_dev(lax.rem(plane + o, NP)), device_id_type=MESH
        )
        return carry

    lax.fori_loop(1, NS, greet, 0)
    pl.semaphore_signal(barrier, inc=1, device_id=partner, device_id_type=MESH)

    def copy1(ph, m, src):
        return pltpu.make_async_remote_copy(
            src_ref=s1.at[ph, m], dst_ref=r1.at[ph, src],
            send_sem=ss1.at[ph, m], recv_sem=rs1.at[ph, src],
            device_id=(m, rp), device_id_type=MESH,
        )

    def copy2(ph, j, src):
        return pltpu.make_async_remote_copy(
            src_ref=s2.at[ph, j], dst_ref=r2.at[ph, src],
            send_sem=ss2.at[ph, j], recv_sem=rs2.at[ph, src],
            device_id=(j, rp), device_id_type=MESH,
        )

    def over_space(fn):
        def step(o, carry):
            fn(lax.rem(sp + o, NS))
            return carry

        lax.fori_loop(1, NS, step, 0)

    def exchange_out(ph, edges):
        for t in range(T):
            top, bottom, left, right = edges(t)
            for d, line in enumerate((bottom, top, right, left)):
                line = line.astype(BF)
                for q in range(4):
                    s1[ph, 4 * d + q, t] = line[16 * q : 16 * q + 16]
            for k, cell in enumerate((bottom[H - 1 :], bottom[:1], top[H - 1 :], top[:1])):
                cfr[NS, pl.ds(t * 4 + k, 1), :] = cell
        block = cfr[NS].astype(BF)
        for m in range(NS):
            s1[ph, m, T] = block
        r1[ph, sp] = s1[ph, sp]

    def exchange_send1(ph):
        over_space(lambda m: copy1(ph, m, sp).start())

    def exchange_route(ph):
        over_space(lambda i: copy1(ph, i, i).wait_recv())
        mine = lax.div(sp, 4)

        def route(j, carry):
            for u in range(T):
                s = slots_s[mine, T * j + u]
                s2[ph, j, u] = r1[ph, lax.div(s, 2), lax.rem(s, 2)]
            return carry

        lax.fori_loop(0, NS, route, 0)
        over_space(lambda j: copy2(ph, j, sp).start())
        r2[ph, sp] = s2[ph, sp]
        cfr[NS] = jnp.zeros((16, C), F32)

        def widen(i, carry):
            cfr[i] = r1[ph, i, T].astype(F32)
            return carry

        lax.fori_loop(0, NS, widen, 0)

    def exchange_in(ph, frame):
        for t in range(T):
            for k, (row, col) in enumerate(
                ((0, WEST), (0, EAST), (H + 1, WEST), (H + 1, EAST))
            ):
                s = slots_s[DIRS + k, T * sp + t]
                frame[t, pl.ds(row * PITCH + col, 1), :] = cfr[
                    lax.div(s, 2), pl.ds(lax.rem(s, 2) * 4 + k, 1), :
                ]
        over_space(lambda i: copy2(ph, i, i).wait_recv())
        for t in range(T):
            for q in range(4):
                frame[t, pl.ds(FIRST + 16 * q, 16), :] = r2[ph, q, t].astype(F32)
                frame[t, pl.ds((H + 1) * PITCH + FIRST + 16 * q, 16), :] = r2[
                    ph, 4 + q, t
                ].astype(F32)
                for d, col in ((2, WEST), (3, EAST)):
                    frame[t, pl.ds((16 * q + 1) * PITCH + col, 16, stride=PITCH), :] = r2[
                        ph, 4 * d + q, t
                    ].astype(F32)

    def exchange_end(ph):
        over_space(lambda m: copy1(ph, m, sp).wait_send())
        over_space(lambda m: copy2(ph, m, sp).wait_send())

    def column(x):
        return pl.ds(PITCH + FIRST + x, H, stride=PITCH)

    for t in range(T):
        load_h(t).wait()

        def fill(y, carry):
            fh[t, pl.ds(at80(y + 1, FIRST), H), :] = hv[t, y].astype(F32)
            return carry

        lax.fori_loop(0, H, fill, 0)
    cfr[NS] = jnp.zeros((16, C), F32)
    exchange_out(
        0,
        lambda t: (
            hv[t, 0].astype(F32), hv[t, H - 1].astype(F32),
            fh[t, column(0), :], fh[t, column(H - 1), :],
        ),
    )
    pl.semaphore_wait(barrier, 2 * (NS - 1) + 1)
    exchange_send1(0)

    own = jnp.broadcast_to(owners[...], (2 * DIRS, 2 * NS))
    near = jnp.full((2 * DIRS, 2 * NS), -1, jnp.int32)
    for tile in range(2 * NS):
        near = jnp.where(own == tile, neigh[:, tile : tile + 1], near)
    found = jnp.full((2 * DIRS, 2 * NS), 2 * NS, jnp.int32)
    for slot in range(2 * NS):
        found = jnp.where(near == owners_s[0, slot], slot, found)
    slots_v[:, 0 : 2 * NS] = found
    to_smem = pltpu.make_async_copy(slots_v, slots_s, lsem.at[2 * T])
    to_smem.start()

    zeros = jnp.zeros((C, C), BF)
    for r in range(4):
        for b in range(3):
            for q in range(2):
                a = r - q
                rows, cols = pl.ds((r * 3 + b) * C, C), pl.ds(q * C, C)
                if 0 <= a <= 2:
                    w4[rows, cols] = weight[a, b]
                else:
                    w4[rows, cols] = zeros
    line = lax.broadcasted_iota(jnp.int32, (C, 2 * C), 0)
    lane = lax.broadcasted_iota(jnp.int32, (C, 2 * C), 1)
    w4[12 * C : 13 * C, :] = jnp.where((line < H) == (lane < C), -OFF, 0.0).astype(BF)
    bacc[...] = jnp.zeros_like(bacc)
    acc[...] = jnp.zeros_like(acc)
    for i in range(2):
        r1[i, NS] = jnp.zeros((3, 16, C), BF)
    for t in range(T):
        for p in range(H // 2):
            got = (1 - tissue[t : t + 1, p * C : (p + 1) * C]).astype(F32)
            raw2[t, 2 * p : 2 * p + 1, :] = got
            raw2[t, 2 * p + 1 : 2 * p + 2, :] = got
            drops[t, p : p + 1, :] = got
    prow = lax.broadcasted_iota(jnp.int32, (H // 2, C), 0)
    plane_lane = lax.broadcasted_iota(jnp.int32, (H // 2, C), 1)
    outer = (
        (plane_lane % H == 0)
        | (plane_lane % H == H - 1)
        | ((prow == 0) & (plane_lane < H))
        | ((prow == H // 2 - 1) & (plane_lane >= H))
    )
    for t in range(T):
        drops[t] = jnp.where(outer, 1.0, drops[t])
    for frame in (fh, fg):
        for t in range(T):
            frame[t, 0:PITCH, :] = jnp.zeros((PITCH, C), F32)
            frame[t, (H + 1) * PITCH : (H + 2) * PITCH, :] = jnp.zeros((PITCH, C), F32)
            frame[t, column(-1), :] = jnp.zeros((H, C), F32)
            frame[t, column(H), :] = jnp.zeros((H, C), F32)
    to_smem.wait()

    def shifts(dst, frame, t):
        def step(y, carry):
            for b in range(3):
                dst[t, y, :, b * C : (b + 1) * C] = frame[
                    t, pl.ds(at80(y, WEST + b), H), :
                ].astype(BF)
            return carry

        lax.fori_loop(0, H + 2, step, 0, unroll=2)

    nb = (H // 2) // PB
    bias2 = jnp.concatenate([bias[...], bias[...]], axis=1)
    sub = lax.broadcasted_iota(jnp.int32, (H, C), 0)
    lanes = lax.broadcasted_iota(jnp.int32, (H, C), 1)
    eye = sub == lanes % H

    def window(src, t, p):
        return jnp.concatenate([src[t, 2 * p + r] for r in range(4)], axis=1)

    def activate(pre):
        sigma = 0.5 * jnp.tanh(0.5 * pre) + 0.5
        act = pre * sigma
        return act, sigma + act * (1.0 - sigma)

    def forward(t):
        def step(i, carry):
            p0 = i * PB
            parts = []
            for k in range(PB):
                drop = jnp.where(eye, drops[t, pl.ds(p0 + k, 1), :], 0.0).astype(BF)
                parts.append(jnp.concatenate([window(x3, t, p0 + k), drop], axis=1))
            pre = jnp.dot(
                jnp.concatenate(parts, axis=0), w4[...], preferred_element_type=F32
            ) + bias2
            act, slope = activate(pre)
            total = jnp.zeros((8, C), F32)
            for k in range(PB):
                for q in range(2):
                    y = 2 * (p0 + k) + q
                    rows, cols = slice(k * H, (k + 1) * H), slice(q * C, (q + 1) * C)
                    fv[t, y] = act[rows, cols].astype(BF)
                    wide = cv[t, y].astype(F32)
                    cotb[t, 2, pl.ds(y, 1), :] = wide[:1]
                    cotb[t, 3, pl.ds(y, 1), :] = wide[H - 1 :]
                    g = (wide * slope[rows, cols]).astype(BF)
                    gv[t, y] = g
                    wide = g.astype(F32)
                    fg[t, pl.ds(at80(y + 1, FIRST), H), :] = wide
                    total = total + jnp.sum(wide.reshape(H // 8, 8, C), axis=0)
            bacc[...] += total
            return carry

        lax.fori_loop(0, nb, step, 0)

    def weights(t):
        def step(i, carry):
            p0 = i * WB
            left = jnp.concatenate(
                [
                    jnp.concatenate(
                        [gv[t, 2 * (p0 + k) + q] for k in range(WB)], axis=0
                    ).astype(F32).T.astype(BF)
                    for q in range(2)
                ],
                axis=0,
            )
            right = jnp.concatenate([window(x3, t, p0 + k) for k in range(WB)], axis=0)
            acc[...] += jnp.dot(left, right, preferred_element_type=F32)
            return carry

        lax.fori_loop(0, (H // 2) // WB, step, 0)

    def backward(t):
        def step(i, carry):
            p0 = i * PB
            got = jnp.dot(
                jnp.concatenate([window(g3, t, p0 + k) for k in range(PB)], axis=0),
                w4g[...],
                preferred_element_type=F32,
            )
            for k in range(PB):
                for q in range(2):
                    iv[t, 2 * (p0 + k) + q] = got[
                        k * H : (k + 1) * H, q * C : (q + 1) * C
                    ].astype(BF)
            return carry

        lax.fori_loop(0, nb, step, 0)

    def patches(frame):
        for t in range(T):
            for side in range(4):
                rows = slice((t * 4 + side) * H, (t * 4 + side + 1) * H)
                y0 = H - 1 if side == 1 else 0
                x0 = H - 1 if side == 3 else 0
                stride = PITCH if side >= 2 else None
                for a in range(3):
                    for b in range(3):
                        got = frame[t, pl.ds((y0 + a) * PITCH + WEST + x0 + b, H, stride=stride), :]
                        tap = a * 3 + b
                        pb[rows, tap * C : (tap + 1) * C] = got.astype(BF)

    def put_columns(dst, src, t):
        low = lax.broadcasted_iota(jnp.int32, (16, C), 0) == 0
        high = lax.broadcasted_iota(jnp.int32, (16, C), 0) == 15

        def step(y, carry):
            first = dst[t, y, 0:16, :].astype(F32)
            dst[t, y, 0:16, :] = jnp.where(low, src[t, 2, pl.ds(y, 1), :], first).astype(BF)
            last = dst[t, y, H - 16 : H, :].astype(F32)
            dst[t, y, H - 16 : H, :] = jnp.where(
                high, src[t, 3, pl.ds(y, 1), :], last
            ).astype(BF)
            return carry

        lax.fori_loop(0, H, step, 0, unroll=4)

    def put_rows(dst, src, t):
        dst[t, 0] = src[t, 0].astype(BF)
        dst[t, H - 1] = src[t, 1].astype(BF)

    copy_a = pltpu.make_async_remote_copy(
        src_ref=arb.at[1 - core], dst_ref=arcv, send_sem=sa, recv_sem=ra,
        device_id=partner, device_id_type=MESH,
    )

    def chunk(p):
        return pl.ds(pl.multiple_of(p * CH, 8), CH)

    def copy_b(p, src):
        return pltpu.make_async_remote_copy(
            src_ref=half.at[chunk(p)], dst_ref=brcv.at[src],
            send_sem=sb.at[p], recv_sem=rb.at[src],
            device_id=plane_dev(p), device_id_type=MESH,
        )

    def copy_c(k, src):
        return pltpu.make_async_remote_copy(
            src_ref=csrc, dst_ref=crcv.at[src], send_sem=sc.at[k], recv_sem=rc.at[src],
            device_id=z_dev(k), device_id_type=MESH,
        )

    def copy_d(p, src):
        return pltpu.make_async_remote_copy(
            src_ref=dsrc, dst_ref=dall.at[chunk(src)], send_sem=sd.at[p], recv_sem=rd.at[src],
            device_id=plane_dev(p), device_id_type=MESH,
        )

    copy_e = pltpu.make_async_remote_copy(
        src_ref=dall, dst_ref=erc, send_sem=se, recv_sem=re,
        device_id=partner, device_id_type=MESH,
    )

    def over_plane(fn):
        def step(o, carry):
            fn(lax.rem(plane + o, NP))
            return carry

        lax.fori_loop(1, NP, step, 0)

    def over_z(fn):
        def step(o, carry):
            fn(lax.rem(z + o, NZ))
            return carry

        lax.fori_loop(1, NZ, step, 0)

    def stage_b():
        copy_a.wait_recv()
        half[...] = arb[core] + arcv[...]
        over_plane(lambda p: copy_b(p, plane).start())
        brcv[plane] = half[chunk(plane)]

    def stage_c():
        over_plane(lambda p: copy_b(p, p).wait_recv())
        total = brcv[0]
        for p in range(1, NP):
            total = total + brcv[p]
        csrc[...] = total
        over_z(lambda k: copy_c(k, z).start())
        crcv[z] = total

    def stage_d():
        over_z(lambda k: copy_c(k, k).wait_recv())
        total = crcv[0]
        for k in range(1, NZ):
            total = total + crcv[k]
        total = total * float(NS * NR * T * H * H) ** -0.5
        dsrc[...] = total
        over_plane(lambda p: copy_d(p, plane).start())
        dall[chunk(plane)] = total

    def stage_e():
        over_plane(lambda p: copy_d(p, p).wait_recv())
        copy_e.start()

    def put_gradient(tap, block, add):
        def put(i, lo, size, val):
            rows = slice(lo, lo + size)
            arb[i, rows] = arb[i, rows] + val if add else val

        if tap < 4:
            put(0, tap * C, C, block)
        elif tap == 4:
            put(0, 4 * C, H, block[:H])
            put(1, 0, H, block[H:])
        else:
            put(1, H + (tap - 5) * C, C, block)

    shifts(x3, fh, 0)
    for t in range(T):
        load_c(t).wait()
    forward(0)
    exchange_route(0)
    shifts(x3, fh, 1)
    forward(1)
    weights(0)
    weights(1)
    for tap in range(9):
        a, b = tap // 3, tap % 3
        w9[tap * C : (tap + 1) * C, :] = weight[a, b]
        lo = slice((a * 3 + b) * C, (a * 3 + b + 1) * C)
        hi = slice(((a + 1) * 3 + b) * C, ((a + 1) * 3 + b + 1) * C)
        put_gradient(tap, (acc[0:C, lo] + acc[C : 2 * C, hi]).T, False)
    w9[9 * C : 10 * C, :] = jnp.full((C, C), -OFF, BF)
    for t in range(T):
        cotb[t, 0] = cv[t, 0].astype(F32)
        cotb[t, 1] = cv[t, H - 1].astype(F32)
        for side, keep in enumerate(
            (
                jnp.where(lanes == sub, raw2[t, 0:1, :], 0.0),
                jnp.where(lanes == sub + H, raw2[t, H - 1 : H, :], 0.0),
                jnp.where(lanes == sub % 2 * H, raw2[t], 0.0),
                jnp.where(lanes == sub % 2 * H + H - 1, raw2[t], 0.0),
            )
        ):
            rows = slice((t * 4 + side) * H, (t * 4 + side + 1) * H)
            pb[rows, 9 * C : 10 * C] = keep.astype(BF)

    exchange_in(0, fh)
    patches(fh)
    pre = jnp.dot(pb[...], w9[...], preferred_element_type=F32) + bias[...]
    act, slope = activate(pre)
    fb[...] = act.reshape(T, 4, H, C)
    grads = (cotb[...].reshape(T * 4 * H, C) * slope).astype(BF).astype(F32)
    gb[...] = grads.reshape(T, 4, H, C)
    spot = lax.broadcasted_iota(jnp.int32, (T * 4 * H, C), 0)
    once = (spot % (4 * H) < 2 * H) | ((spot % H > 0) & (spot % H < H - 1))
    grads = jnp.where(once, grads, 0.0)
    outer_w = jnp.dot(
        grads.T.astype(BF), pb[:, 0 : 9 * C], preferred_element_type=F32
    )
    for tap in range(9):
        put_gradient(tap, outer_w[:, tap * C : (tap + 1) * C].T, True)
    bsum = jnp.sum(bacc[...], axis=0, keepdims=True) + jnp.sum(grads, axis=0, keepdims=True)
    first = lax.broadcasted_iota(jnp.int32, (HALF - 576, C), 0) == 0
    for i in range(2):
        arb[i, 576:HALF] = jnp.where(first, bsum, 0.0)
    copy_a.start()

    cfr[NS] = jnp.zeros((16, C), F32)
    exchange_out(1, lambda t: tuple(gb[t, side] for side in range(4)))
    exchange_send1(1)
    stage_b()

    for t in range(T):
        put_rows(fv, fb, t)
        put_columns(fv, fb, t)
        fg[t, pl.ds(PITCH + FIRST, H), :] = gb[t, 0]
        fg[t, pl.ds(H * PITCH + FIRST, H), :] = gb[t, 1]
        fg[t, column(0), :] = gb[t, 2]
        fg[t, column(H - 1), :] = gb[t, 3]
    out_f = pltpu.make_async_copy(fv, feat, osem.at[0])
    out_f.start()
    for r in range(4):
        for b in range(3):
            for q in range(2):
                a = r - q
                rows, cols = pl.ds((r * 3 + b) * C, C), pl.ds(q * C, C)
                if 0 <= a <= 2:
                    turned = weight[2 - a, 2 - b].astype(F32).T.astype(BF)
                    w4g[rows, cols] = turned
                    if q == 0:
                        w9g[(a * 3 + b) * C : (a * 3 + b + 1) * C, :] = turned
                else:
                    w4g[rows, cols] = zeros
    shifts(g3, fg, 0)
    shifts(g3, fg, 1)
    exchange_route(1)
    stage_c()
    backward(0)
    backward(1)
    stage_d()

    exchange_in(1, fg)
    patches(fg)
    got = jnp.dot(pb[:, 0 : 9 * C], w9g[...], preferred_element_type=F32)
    fb[...] = got.reshape(T, 4, H, C)
    out_i = []
    for t in range(T):
        put_rows(iv, fb, t)
        put_columns(iv, fb, t)
        out_i.append(pltpu.make_async_copy(iv.at[t], ingrad.at[t], osem.at[1 + t]))
        out_i[t].start()
    stage_e()

    exchange_end(0)
    exchange_end(1)
    copy_a.wait_send()
    over_plane(lambda p: copy_b(p, plane).wait_send())
    over_z(lambda k: copy_c(k, z).wait_send())
    over_plane(lambda p: copy_d(p, plane).wait_send())
    out_f.wait()
    for t in range(T):
        out_i[t].wait()
    copy_e.wait()
    rows_mine = pl.ds(pl.multiple_of(core * 576, 8), 576)
    rows_other = pl.ds(pl.multiple_of((1 - core) * 576, 8), 576)
    packed[rows_mine, :] = dall[0:576]
    packed[rows_other, :] = erc[0:576]
    packed[1152:1160, :] = dall[576:584]


def finish(feat, ingrad, packed, feat_out, ingrad_out, wgrad, bgrad, fv, iv, sem):
    ins = [pltpu.make_async_copy(feat, fv, sem.at[0]), pltpu.make_async_copy(ingrad, iv, sem.at[1])]
    outs = [
        pltpu.make_async_copy(fv, feat_out, sem.at[2]),
        pltpu.make_async_copy(iv, ingrad_out, sem.at[3]),
    ]
    for copy in ins:
        copy.start()
    wgrad[...] = packed[0 : 9 * C]
    bgrad[...] = packed[9 * C : 9 * C + 1]
    for one, other in zip(ins, outs):
        one.wait()
        other.start()
    for copy in outs:
        copy.wait()


def local(hologram, weight, conv_bias, cotangent, tissue, owners, neighbours):
    vmem = pl.BlockSpec(memory_space=pltpu.VMEM)
    smem = pl.BlockSpec(memory_space=pltpu.SMEM)
    hbm = pl.BlockSpec(memory_space=pl.ANY)
    tiles = jax.ShapeDtypeStruct((T, H, H, C), BF)
    dma = pltpu.SemaphoreType.DMA
    feat, ingrad, packed = pl.pallas_call(
        kernel,
        out_shape=(tiles, tiles, jax.ShapeDtypeStruct((9 * C + 8, C), F32)),
        in_specs=[hbm, vmem, vmem, hbm, vmem, vmem, smem, vmem],
        out_specs=(hbm, hbm, vmem),
        scratch_shapes=[
            pltpu.VMEM((T, H, H, C), BF),
            pltpu.VMEM((T, H, H, C), BF),
            pltpu.VMEM((T, H, H, C), BF),
            pltpu.VMEM((T, H, H, C), BF),
            pltpu.VMEM((T, H, H, C), BF),
            pltpu.VMEM((T, (H + 3) * PITCH, C), F32),
            pltpu.VMEM((T, (H + 3) * PITCH, C), F32),
            pltpu.VMEM((T, H + 2, H, 3 * C), BF),
            pltpu.VMEM((T, H + 2, H, 3 * C), BF),
            pltpu.VMEM((13 * C, 2 * C), BF),
            pltpu.VMEM((12 * C, 2 * C), BF),
            pltpu.VMEM((10 * C, C), BF),
            pltpu.VMEM((9 * C, C), BF),
            pltpu.VMEM((T * 4 * H, 10 * C), BF),
            pltpu.VMEM((2 * C, 12 * C), F32),
            pltpu.VMEM((8, C), F32),
            pltpu.VMEM((T, H, C), F32),
            pltpu.VMEM((T, H // 2, C), F32),
            pltpu.VMEM((T, 4, H, C), F32),
            pltpu.VMEM((T, 4, H, C), F32),
            pltpu.VMEM((T, 4, H, C), F32),
            pltpu.VMEM((NS + 1, 16, C), F32),
            pltpu.VMEM((8, C), jnp.int32),
            pltpu.SMEM((8, C), jnp.int32),
            pltpu.VMEM((2, NS, 3, 16, C), BF),
            pltpu.VMEM((2, NS + 1, 3, 16, C), BF),
            pltpu.VMEM((2, NS, T, 16, C), BF),
            pltpu.VMEM((2, NS, T, 16, C), BF),
            pltpu.VMEM((2, HALF, C), F32),
            pltpu.VMEM((HALF, C), F32),
            pltpu.VMEM((HALF, C), F32),
            pltpu.VMEM((NP, CH, C), F32),
            pltpu.VMEM((CH, C), F32),
            pltpu.VMEM((NZ, CH, C), F32),
            pltpu.VMEM((CH, C), F32),
            pltpu.VMEM((HALF, C), F32),
            pltpu.VMEM((HALF, C), F32),
            dma((2 * T + 1,)),
            dma((1 + T,)),
            dma((2, NS)), dma((2, NS)), dma((2, NS)), dma((2, NS)),
            dma, dma,
            dma((NP,)), dma((NP,)),
            dma((NZ,)), dma((NZ,)),
            dma((NP,)), dma((NP,)),
            dma, dma,
        ],
        compiler_params=pltpu.CompilerParams(
            collective_id=0, has_side_effects=True, vmem_limit_bytes=56 * 2**20
        ),
        cost_estimate=pl.CostEstimate(
            flops=7247757312, bytes_accessed=10 * 2**20, transcendentals=2**20
        ),
        name="unet_conv_step",
    )(
        hologram[0], weight, conv_bias[None], cotangent[0], tissue[0], owners, owners,
        neighbours[0],
    )
    feat, ingrad, wgrad, bgrad = pl.pallas_call(
        finish,
        out_shape=(
            tiles,
            tiles,
            jax.ShapeDtypeStruct((9 * C, C), F32),
            jax.ShapeDtypeStruct((1, C), F32),
        ),
        in_specs=[hbm, hbm, vmem],
        out_specs=(hbm, hbm, vmem, vmem),
        scratch_shapes=[
            pltpu.VMEM((T, H, H, C), BF), pltpu.VMEM((T, H, H, C), BF), dma((4,))
        ],
        compiler_params=pltpu.CompilerParams(vmem_limit_bytes=32 * 2**20),
        name="hand_over",
    )(feat, ingrad, packed)
    return (
        feat[None], ingrad[None], wgrad.reshape(3, 3, C, C), bgrad.reshape(C)
    )


def solution(mesh):
    return jax.shard_map(
        local,
        mesh=mesh,
        in_specs=(
            P("replica", "space", None, None, None),
            P(),
            P(),
            P("replica", "space", None, None, None),
            P("replica", "space", None),
            P("replica", None),
            P("replica", None, None),
        ),
        out_specs=(
            P("replica", "space", None, None, None),
            P("replica", "space", None, None, None),
            P(),
            P(),
        ),
        check_vma=False,
    )
```

```python
import functools

import jax
import jax.numpy as jnp
from jax import lax
from jax.experimental import pallas as pl
from jax.experimental.pallas import tpu as pltpu
from jax.sharding import PartitionSpec as P

MESH = pl.DeviceIdType.MESH
BF = jnp.bfloat16
F32 = jnp.float32

NS = 16
NR = 16
NZ = 8
NP = 16
T = 2
H = 64
C = 128
PITCH = 80
WEST, FIRST, EAST = 7, 8, 72
CH = 48
OWNERS = 13
HALF = OWNERS * CH
FAR_Z = (4, 3, 5, 2, 6, 1, 7)
FAR_SPACE = sorted(
    ((dz, dy) for dz in range(8) for dy in range(2) if dz or dy),
    key=lambda d: -min(d[0], 8 - d[0]) - d[1],
)
FAR_PLANE = sorted(
    ((dx, dy) for dx in range(4) for dy in range(4) if dx or dy),
    key=lambda d: -min(d[0], 4 - d[0]) - min(d[1], 4 - d[1]),
)
CORNER_AT = (3, 0, 7, 4)
CORNER_ROW = (15, 0, 15, 0)
OFF = float(2**20)
PB = 16
WB = 32
DIRS = 4


def at80(row, off):
    return pl.multiple_of(row * PITCH, 8) + off


def kernel(
    holo, weight_in, bias_in, cot, tissue_in, owners_in, neigh_in,
    fv, iv, packed,
    weight, bias, tissue, owners, owners_s, neigh,
    hv, cv, gv, fh, fg, x3, w4, w4g, w9, w9g, pb, acc, bacc, raw2, drops,
    cotb, fb, gb, slots_v, slots_s,
    s1, r1a, r1b, s2, r2, s3, r3, arb, ah, arcv, half, brcv, csrc, crcv, dsrc, dall, erc,
    lsem, ss1, rs1, ss2, rs2, ss3, rs3, sa, ra, sb, rb, sc, rc, sd, rd, se, re,
):
    sp = lax.axis_index("space")
    rp = lax.axis_index("replica")
    z, ylo = lax.div(sp, 2), lax.rem(sp, 2)
    core = lax.rem(rp, 2)
    plane = lax.div(rp, 4) * 4 + lax.rem(lax.div(rp, 2), 2) * 2 + ylo

    def plane_dev(p):
        return (z * 2 + lax.rem(p, 2), lax.div(p, 2) * 2 + core)

    def z_dev(k):
        return (k * 2 + ylo, rp)

    partner = (sp, rp + 1 - 2 * core)
    r1 = (r1a, r1b)

    barrier = pltpu.get_barrier_semaphore()

    def near_space(d):
        return lax.rem(z + d[0], NZ) * 2 + lax.rem(ylo + d[1], 2)

    def near_plane(d):
        return lax.rem(lax.div(plane, 4) + d[0], 4) * 4 + lax.rem(lax.rem(plane, 4) + d[1], 4)

    for d in FAR_SPACE:
        pl.semaphore_signal(
            barrier, inc=1, device_id=(near_space(d), rp), device_id_type=MESH
        )
    for d in FAR_PLANE:
        pl.semaphore_signal(
            barrier, inc=1, device_id=plane_dev(near_plane(d)), device_id_type=MESH
        )
    pl.semaphore_signal(barrier, inc=1, device_id=partner, device_id_type=MESH)

    def load_h(t):
        return pltpu.make_async_copy(holo.at[t], hv.at[t], lsem.at[t])

    def load_c(t):
        return pltpu.make_async_copy(cot.at[t], cv.at[t], lsem.at[T + t])

    small = [
        pltpu.make_async_copy(src, dst, lsem.at[2 * T + 1 + i])
        for i, (src, dst) in enumerate(
            (
                (owners_in, owners), (owners_in, owners_s), (neigh_in, neigh),
                (tissue_in, tissue), (bias_in, bias), (weight_in, weight),
            )
        )
    ]
    for t in range(T):
        load_h(t).start()
    for copy in small:
        copy.start()
    for t in range(T):
        load_c(t).start()

    def copy1(ph, m, src):
        return pltpu.make_async_remote_copy(
            src_ref=s1.at[ph, m], dst_ref=r1[ph].at[src],
            send_sem=ss1.at[ph], recv_sem=rs1.at[ph],
            device_id=(m, rp), device_id_type=MESH,
        )

    def copy2(ph, j, src):
        return pltpu.make_async_remote_copy(
            src_ref=s2.at[ph, j], dst_ref=r2.at[ph, src],
            send_sem=ss2.at[ph], recv_sem=rs2.at[ph],
            device_id=(j, rp), device_id_type=MESH,
        )

    def copy3(ph, j, k):
        return pltpu.make_async_remote_copy(
            src_ref=s3.at[ph, j], dst_ref=r3.at[ph, k],
            send_sem=ss3.at[ph], recv_sem=rs3.at[ph, k],
            device_id=(j, rp), device_id_type=MESH,
        )

    def step(src_ref, dst_ref, send_sem, recv_sem):
        return pltpu.make_async_remote_copy(
            src_ref=src_ref, dst_ref=dst_ref, send_sem=send_sem, recv_sem=recv_sem,
            device_id=partner, device_id_type=MESH,
        )

    others = pl.ds(0, NS - 1)

    def step1(ph):
        return step(s1.at[ph, others], r1[ph].at[others], ss1.at[ph], rs1.at[ph])

    def step2(ph):
        return step(s2.at[ph, others], r2.at[ph, others], ss2.at[ph], rs2.at[ph])

    def far_space(fn):
        for d in FAR_SPACE:
            fn(near_space(d))

    def over_space(fn):
        def step(o, carry):
            fn(lax.rem(sp + o, NS))
            return carry

        lax.fori_loop(1, NS, step, 0)

    def exchange_out(ph, edges):
        for t in range(T):
            top, bottom, left, right = edges(t)
            for d, line in enumerate((bottom, top, right, left)):
                line = line.astype(BF)
                for q in range(4):
                    s1[ph, 4 * d + q, t] = line[16 * q : 16 * q + 16]
        r1[ph][sp] = s1[ph, sp]

    def exchange_send1(ph):
        far_space(lambda m: copy1(ph, m, sp).start())

    def exchange_route(ph):
        step1(ph).wait_recv()
        mine = lax.div(sp, 4)

        def route(j):
            for u in range(T):
                s = slots_s[mine, T * j + u]
                s2[ph, j, u] = r1[ph][lax.div(s, 2), lax.rem(s, 2)]

        def send(j):
            route(j)
            copy2(ph, j, sp).start()

        far_space(send)
        route(sp)
        r2[ph, sp] = s2[ph, sp]
        for k in range(DIRS):

            @pl.when(sp == CORNER_AT[k])
            def _():
                def corner(j):
                    for u in range(T):
                        s = slots_s[DIRS + k, T * j + u]
                        cells = r1[ph][lax.div(s, 2), lax.rem(s, 2)].astype(F32)
                        s3[ph, j, u : u + 1] = cells[CORNER_ROW[k] : CORNER_ROW[k] + 1]

                def give(j):
                    corner(j)
                    copy3(ph, j, k).start()

                over_space(give)
                corner(sp)
                r3[ph, k] = s3[ph, sp]

    def exchange_in(ph, frame):
        step2(ph).wait_recv()
        for t in range(T):
            for q in range(4):
                frame[t, pl.ds(FIRST + 16 * q, 16), :] = r2[ph, q, t].astype(F32)
                frame[t, pl.ds((H + 1) * PITCH + FIRST + 16 * q, 16), :] = r2[
                    ph, 4 + q, t
                ].astype(F32)
                for d, col in ((2, WEST), (3, EAST)):
                    frame[t, pl.ds((16 * q + 1) * PITCH + col, 16, stride=PITCH), :] = r2[
                        ph, 4 * d + q, t
                    ].astype(F32)
        for k in range(DIRS):

            @pl.when(sp != CORNER_AT[k])
            def _():
                copy3(ph, CORNER_AT[k], k).wait_recv()

        for t in range(T):
            for k, (row, col) in enumerate(
                ((0, WEST), (0, EAST), (H + 1, WEST), (H + 1, EAST))
            ):
                frame[t, pl.ds(row * PITCH + col, 1), :] = r3[ph, k, t : t + 1]

    def exchange_end(ph):
        step1(ph).wait_send()
        step2(ph).wait_send()
        for k in range(DIRS):

            @pl.when(sp == CORNER_AT[k])
            def _():
                step(
                    s3.at[ph, others], s3.at[ph, others], ss3.at[ph], rs3.at[ph, k]
                ).wait_send()

    def column(x):
        return pl.ds(PITCH + FIRST + x, H, stride=PITCH)

    for t in range(T):
        load_h(t).wait()

        def fill(y, carry):
            fh[t, pl.ds(at80(y + 1, FIRST), H), :] = hv[t, y].astype(F32)
            return carry

        lax.fori_loop(0, H, fill, 0)
    exchange_out(
        0,
        lambda t: (
            hv[t, 0].astype(F32), hv[t, H - 1].astype(F32),
            fh[t, column(0), :], fh[t, column(H - 1), :],
        ),
    )
    pl.semaphore_wait(barrier, 2 * (NS - 1) + 1)
    exchange_send1(0)

    for copy in small:
        copy.wait()

    own = jnp.broadcast_to(owners[...], (2 * DIRS, 2 * NS))
    near = jnp.full((2 * DIRS, 2 * NS), -1, jnp.int32)
    for tile in range(2 * NS):
        near = jnp.where(own == tile, neigh[:, tile : tile + 1], near)
    found = jnp.full((2 * DIRS, 2 * NS), 2 * NS, jnp.int32)
    for slot in range(2 * NS):
        found = jnp.where(near == owners_s[0, slot], slot, found)
    slots_v[:, 0 : 2 * NS] = found
    to_smem = pltpu.make_async_copy(slots_v, slots_s, lsem.at[2 * T])
    to_smem.start()

    zeros = jnp.zeros((C, C), BF)
    for r in range(4):
        for b in range(3):
            for q in range(2):
                a = r - q
                rows, cols = pl.ds((r * 3 + b) * C, C), pl.ds(q * C, C)
                if 0 <= a <= 2:
                    w4[rows, cols] = weight[a, b]
                else:
                    w4[rows, cols] = zeros
    line = lax.broadcasted_iota(jnp.int32, (C, 2 * C), 0)
    lane = lax.broadcasted_iota(jnp.int32, (C, 2 * C), 1)
    w4[12 * C : 13 * C, :] = jnp.where((line < H) == (lane < C), -OFF, 0.0).astype(BF)
    bacc[...] = jnp.zeros_like(bacc)
    acc[...] = jnp.zeros_like(acc)
    for i in range(2):
        r1[i][NS] = jnp.zeros((T, 16, C), BF)
    for t in range(T):
        for p in range(H // 2):
            got = (1 - tissue[t : t + 1, p * C : (p + 1) * C]).astype(F32)
            raw2[t, 2 * p : 2 * p + 1, :] = got
            raw2[t, 2 * p + 1 : 2 * p + 2, :] = got
            drops[t, p : p + 1, :] = got
    prow = lax.broadcasted_iota(jnp.int32, (H // 2, C), 0)
    plane_lane = lax.broadcasted_iota(jnp.int32, (H // 2, C), 1)
    outer = (
        (plane_lane % H == 0)
        | (plane_lane % H == H - 1)
        | ((prow == 0) & (plane_lane < H))
        | ((prow == H // 2 - 1) & (plane_lane >= H))
    )
    for t in range(T):
        drops[t] = jnp.where(outer, 1.0, drops[t])
    for frame in (fh, fg):
        for t in range(T):
            frame[t, 0:PITCH, :] = jnp.zeros((PITCH, C), F32)
            frame[t, (H + 1) * PITCH : (H + 2) * PITCH, :] = jnp.zeros((PITCH, C), F32)
            frame[t, column(-1), :] = jnp.zeros((H, C), F32)
            frame[t, column(H), :] = jnp.zeros((H, C), F32)
    to_smem.wait()

    def shifts(dst, frame, t):
        def step(y, carry):
            for b in range(3):
                dst[t, y, :, b * C : (b + 1) * C] = frame[
                    t, pl.ds(at80(y, WEST + b), H), :
                ].astype(BF)
            return carry

        lax.fori_loop(0, H + 2, step, 0, unroll=2)

    nb = (H // 2) // PB
    bias2 = jnp.concatenate([bias[...], bias[...]], axis=1)
    sub = lax.broadcasted_iota(jnp.int32, (H, C), 0)
    lanes = lax.broadcasted_iota(jnp.int32, (H, C), 1)
    eye = sub == lanes % H

    def window(src, t, p):
        return jnp.concatenate([src[t, 2 * p + r] for r in range(4)], axis=1)

    def activate(pre):
        sigma = 0.5 * jnp.tanh(0.5 * pre) + 0.5
        act = pre * sigma
        return act, sigma + act * (1.0 - sigma)

    def forward(t):
        def step(i, carry):
            p0 = i * PB
            parts = []
            for k in range(PB):
                drop = jnp.where(eye, drops[t, pl.ds(p0 + k, 1), :], 0.0).astype(BF)
                parts.append(jnp.concatenate([window(x3, t, p0 + k), drop], axis=1))
            pre = jnp.dot(
                jnp.concatenate(parts, axis=0), w4[...], preferred_element_type=F32
            ) + bias2
            act, slope = activate(pre)
            total = jnp.zeros((8, C), F32)
            for k in range(PB):
                for q in range(2):
                    y = 2 * (p0 + k) + q
                    rows, cols = slice(k * H, (k + 1) * H), slice(q * C, (q + 1) * C)
                    fv[t, y] = act[rows, cols].astype(BF)
                    wide = cv[t, y].astype(F32)
                    cotb[t, 2, pl.ds(y, 1), :] = wide[:1]
                    cotb[t, 3, pl.ds(y, 1), :] = wide[H - 1 :]
                    g = (wide * slope[rows, cols]).astype(BF)
                    gv[t, y] = g
                    wide = g.astype(F32)
                    fg[t, pl.ds(at80(y + 1, FIRST), H), :] = wide
                    total = total + jnp.sum(wide.reshape(H // 8, 8, C), axis=0)
            bacc[...] += total
            return carry

        lax.fori_loop(0, nb, step, 0)

    def weights(t):
        def step(i, carry):
            p0 = i * WB
            left = jnp.concatenate(
                [
                    jnp.concatenate(
                        [gv[t, 2 * (p0 + k) + q] for k in range(WB)], axis=0
                    ).astype(F32).T.astype(BF)
                    for q in range(2)
                ],
                axis=0,
            )
            right = jnp.concatenate([window(x3, t, p0 + k) for k in range(WB)], axis=0)
            acc[...] += jnp.dot(left, right, preferred_element_type=F32)
            return carry

        lax.fori_loop(0, (H // 2) // WB, step, 0)

    def backward(t):
        def step(i, carry):
            p0 = i * PB
            got = jnp.dot(
                jnp.concatenate([window(x3, t, p0 + k) for k in range(PB)], axis=0),
                w4g[...],
                preferred_element_type=F32,
            )
            for k in range(PB):
                for q in range(2):
                    iv[t, 2 * (p0 + k) + q] = got[
                        k * H : (k + 1) * H, q * C : (q + 1) * C
                    ].astype(BF)
            return carry

        lax.fori_loop(0, nb, step, 0)

    def patches(frame):
        for t in range(T):
            for side in range(4):
                rows = slice((t * 4 + side) * H, (t * 4 + side + 1) * H)
                y0 = H - 1 if side == 1 else 0
                x0 = H - 1 if side == 3 else 0
                stride = PITCH if side >= 2 else None
                for a in range(3):
                    for b in range(3):
                        got = frame[t, pl.ds((y0 + a) * PITCH + WEST + x0 + b, H, stride=stride), :]
                        tap = a * 3 + b
                        pb[rows, tap * C : (tap + 1) * C] = got.astype(BF)

    def put_columns(dst, src, t):
        low = lax.broadcasted_iota(jnp.int32, (16, C), 0) == 0
        high = lax.broadcasted_iota(jnp.int32, (16, C), 0) == 15

        def step(y, carry):
            first = dst[t, y, 0:16, :].astype(F32)
            dst[t, y, 0:16, :] = jnp.where(low, src[t, 2, pl.ds(y, 1), :], first).astype(BF)
            last = dst[t, y, H - 16 : H, :].astype(F32)
            dst[t, y, H - 16 : H, :] = jnp.where(
                high, src[t, 3, pl.ds(y, 1), :], last
            ).astype(BF)
            return carry

        lax.fori_loop(0, H, step, 0, unroll=4)

    def put_rows(dst, src, t):
        dst[t, 0] = src[t, 0].astype(BF)
        dst[t, H - 1] = src[t, 1].astype(BF)

    copy_a = pltpu.make_async_remote_copy(
        src_ref=ah, dst_ref=arcv, send_sem=sa, recv_sem=ra,
        device_id=partner, device_id_type=MESH,
    )

    def chunk(p):
        return pl.ds(pl.multiple_of(p * CH, 16), CH)

    def copy_b(p, src):
        return pltpu.make_async_remote_copy(
            src_ref=half.at[chunk(p)], dst_ref=brcv.at[src],
            send_sem=sb, recv_sem=rb,
            device_id=plane_dev(p), device_id_type=MESH,
        )

    def copy_c(k, src):
        return pltpu.make_async_remote_copy(
            src_ref=csrc, dst_ref=crcv.at[src], send_sem=sc, recv_sem=rc,
            device_id=z_dev(k), device_id_type=MESH,
        )

    def copy_d(p, src):
        return pltpu.make_async_remote_copy(
            src_ref=dsrc, dst_ref=dall.at[chunk(src)], send_sem=sd, recv_sem=rd,
            device_id=plane_dev(p), device_id_type=MESH,
        )

    copy_e = pltpu.make_async_remote_copy(
        src_ref=dall, dst_ref=erc, send_sem=se, recv_sem=re,
        device_id=partner, device_id_type=MESH,
    )

    in_plane, in_ring = pl.ds(0, NP - 1), pl.ds(0, NZ - 1)

    def step_b(rows):
        return step(half.at[pl.ds(0, rows)], brcv.at[in_plane], sb, rb)

    def step_c():
        return step(crcv.at[in_ring], crcv.at[in_ring], sc, rc)

    def step_d(rows):
        return step(brcv.at[in_plane], dall.at[pl.ds(0, rows)], sd, rd)

    owner = plane < OWNERS

    def stage_a():
        ah[...] = arb[1 - core].astype(BF)
        copy_a.start()

    def stage_b():
        copy_a.wait_recv()
        half[...] = (arb[core] + arcv[...].astype(F32)).astype(BF)
        for d in FAR_PLANE:
            p = near_plane(d)
            pl.when(p < OWNERS)(lambda p=p: copy_b(p, plane).start())

        @pl.when(owner)
        def _():
            brcv[plane] = half[chunk(plane)]

    def stage_c():
        @pl.when(owner)
        def _():
            step_b(HALF).wait_recv()
            total = brcv[0].astype(F32)
            for p in range(1, NP):
                total = total + brcv[p].astype(F32)
            csrc[...] = total.astype(BF)
            for d in FAR_Z:
                copy_c(lax.rem(z + d, NZ), z).start()
            crcv[z] = csrc[...]

    def stage_d():
        @pl.when(owner)
        def _():
            step_c().wait_recv()
            total = crcv[0].astype(F32)
            for k in range(1, NZ):
                total = total + crcv[k].astype(F32)
            dsrc[...] = (total * float(NS * NR * T * H * H) ** -0.5).astype(BF)
            for d in FAR_PLANE:
                copy_d(near_plane(d), plane).start()
            dall[chunk(plane)] = dsrc[...]

    def stage_e():
        @pl.when(owner)
        def _():
            step_d(HALF - CH).wait_recv()

        @pl.when(jnp.logical_not(owner))
        def _():
            step_d(HALF).wait_recv()

        copy_e.start()

    def put_gradient(tap, block, add):
        def put(i, lo, size, val):
            rows = slice(lo, lo + size)
            arb[i, rows] = arb[i, rows] + val if add else val

        if tap < 4:
            put(0, tap * C, C, block)
        elif tap == 4:
            put(0, 4 * C, H, block[:H])
            put(1, 0, H, block[H:])
        else:
            put(1, H + (tap - 5) * C, C, block)

    shifts(x3, fh, 0)
    for t in range(T):
        load_c(t).wait()
    shifts(x3, fh, 1)
    for tap in range(9):
        a, b = tap // 3, tap % 3
        w9[tap * C : (tap + 1) * C, :] = weight[a, b]
    w9[9 * C : 10 * C, :] = jnp.full((C, C), -OFF, BF)
    for t in range(T):
        cotb[t, 0] = cv[t, 0].astype(F32)
        cotb[t, 1] = cv[t, H - 1].astype(F32)
        for side, keep in enumerate(
            (
                jnp.where(lanes == sub, raw2[t, 0:1, :], 0.0),
                jnp.where(lanes == sub + H, raw2[t, H - 1 : H, :], 0.0),
                jnp.where(lanes == sub % 2 * H, raw2[t], 0.0),
                jnp.where(lanes == sub % 2 * H + H - 1, raw2[t], 0.0),
            )
        ):
            rows = slice((t * 4 + side) * H, (t * 4 + side + 1) * H)
            pb[rows, 9 * C : 10 * C] = keep.astype(BF)

    forward(0)
    exchange_route(0)
    forward(1)
    weights(0)
    weights(1)
    for tap in range(9):
        a, b = tap // 3, tap % 3
        lo = slice((a * 3 + b) * C, (a * 3 + b + 1) * C)
        hi = slice(((a + 1) * 3 + b) * C, ((a + 1) * 3 + b + 1) * C)
        put_gradient(tap, acc[0:C, lo] + acc[C : 2 * C, hi], False)

    exchange_in(0, fh)
    patches(fh)
    pre = jnp.dot(pb[...], w9[...], preferred_element_type=F32) + bias[...]
    act, slope = activate(pre)
    fb[...] = act.reshape(T, 4, H, C)
    grads = (cotb[...].reshape(T * 4 * H, C) * slope).astype(BF).astype(F32)
    gb[...] = grads.reshape(T, 4, H, C)
    spot = lax.broadcasted_iota(jnp.int32, (T * 4 * H, C), 0)
    once = (spot % (4 * H) < 2 * H) | ((spot % H > 0) & (spot % H < H - 1))
    grads = jnp.where(once, grads, 0.0)
    outer_w = jnp.dot(
        grads.T.astype(BF), pb[:, 0 : 9 * C], preferred_element_type=F32
    )
    for tap in range(9):
        put_gradient(tap, outer_w[:, tap * C : (tap + 1) * C], True)
    bsum = jnp.sum(bacc[...], axis=0, keepdims=True) + jnp.sum(grads, axis=0, keepdims=True)
    first = lax.broadcasted_iota(jnp.int32, (HALF - 576, C), 0) == 0
    arb[0, 576:HALF] = jnp.where(first, bsum, 0.0)
    arb[1, 576:HALF] = jnp.zeros((HALF - 576, C), F32)
    stage_a()

    exchange_out(1, lambda t: tuple(gb[t, side] for side in range(4)))
    exchange_send1(1)
    stage_b()

    for t in range(T):
        put_rows(fv, fb, t)
        put_columns(fv, fb, t)
        fg[t, pl.ds(PITCH + FIRST, H), :] = gb[t, 0]
        fg[t, pl.ds(H * PITCH + FIRST, H), :] = gb[t, 1]
        fg[t, column(0), :] = gb[t, 2]
        fg[t, column(H - 1), :] = gb[t, 3]
    for r in range(4):
        for b in range(3):
            for q in range(2):
                a = r - q
                rows, cols = pl.ds((r * 3 + b) * C, C), pl.ds(q * C, C)
                if 0 <= a <= 2:
                    turned = weight[2 - a, 2 - b].astype(F32).T.astype(BF)
                    w4g[rows, cols] = turned
                    if q == 0:
                        w9g[(a * 3 + b) * C : (a * 3 + b + 1) * C, :] = turned
                else:
                    w4g[rows, cols] = zeros
    shifts(x3, fg, 0)
    shifts(x3, fg, 1)
    exchange_route(1)
    stage_c()
    backward(0)
    backward(1)
    stage_d()

    exchange_in(1, fg)
    patches(fg)
    got = jnp.dot(pb[:, 0 : 9 * C], w9g[...], preferred_element_type=F32)
    fb[...] = got.reshape(T, 4, H, C)
    for t in range(T):
        put_rows(iv, fb, t)
        put_columns(iv, fb, t)
    exchange_end(0)
    exchange_end(1)
    copy_a.wait_send()

    @pl.when(owner)
    def _():
        step_b(HALF - CH).wait_send()
        step_c().wait_send()

    @pl.when(jnp.logical_not(owner))
    def _():
        step_b(HALF).wait_send()

    stage_e()

    @pl.when(owner)
    def _():
        step_d(HALF).wait_send()

    packed[core] = dall[...]
    copy_e.wait()
    packed[1 - core] = erc[...]


def finish(feat, ingrad, packed, feat_out, ingrad_out, wgrad_out, bgrad, wgrad, sem):
    copies = [
        pltpu.make_async_copy(feat, feat_out, sem.at[0]),
        pltpu.make_async_copy(ingrad, ingrad_out, sem.at[1]),
        pltpu.make_async_copy(wgrad, wgrad_out, sem.at[2]),
    ]
    for copy in copies[:2]:
        copy.start()
    for tap in range(9):
        if tap < 4:
            block = packed[0, tap * C : (tap + 1) * C]
        elif tap == 4:
            block = jnp.concatenate([packed[0, 4 * C : 4 * C + H], packed[1, 0:H]], axis=0)
        else:
            block = packed[1, H + (tap - 5) * C : H + (tap - 4) * C]
        wgrad[tap * C : (tap + 1) * C, :] = block.astype(F32).T
    copies[2].start()
    bgrad[...] = packed[0, 576 : 576 + 16].astype(F32)[0:1]
    for copy in copies:
        copy.wait()


def local(hologram, weight, conv_bias, cotangent, tissue, owners, neighbours):
    vmem = pl.BlockSpec(memory_space=pltpu.VMEM)
    hbm = pl.BlockSpec(memory_space=pltpu.HBM)
    tiles = jax.ShapeDtypeStruct((T, H, H, C), BF)
    dma = pltpu.SemaphoreType.DMA
    feat, ingrad, packed = pl.pallas_call(
        kernel,
        out_shape=(
            pltpu.VMEM((T, H, H, C), BF),
            pltpu.VMEM((T, H, H, C), BF),
            pltpu.VMEM((2, HALF, C), BF),
        ),
        in_specs=[hbm] * 7,
        out_specs=(vmem, vmem, vmem),
        scratch_shapes=[
            pltpu.VMEM((3, 3, C, C), BF),
            pltpu.VMEM((1, C), F32),
            pltpu.VMEM((T, H * H), jnp.int32),
            pltpu.VMEM((1, 2 * NS), jnp.int32),
            pltpu.SMEM((1, 2 * NS), jnp.int32),
            pltpu.VMEM((2 * DIRS, 2 * NS), jnp.int32),
            pltpu.VMEM((T, H, H, C), BF),
            pltpu.VMEM((T, H, H, C), BF),
            pltpu.VMEM((T, H, H, C), BF),
            pltpu.VMEM((T, (H + 3) * PITCH, C), F32),
            pltpu.VMEM((T, (H + 3) * PITCH, C), F32),
            pltpu.VMEM((T, H + 2, H, 3 * C), BF),
            pltpu.VMEM((13 * C, 2 * C), BF),
            pltpu.VMEM((12 * C, 2 * C), BF),
            pltpu.VMEM((10 * C, C), BF),
            pltpu.VMEM((9 * C, C), BF),
            pltpu.VMEM((T * 4 * H, 10 * C), BF),
            pltpu.VMEM((2 * C, 12 * C), F32),
            pltpu.VMEM((8, C), F32),
            pltpu.VMEM((T, H, C), F32),
            pltpu.VMEM((T, H // 2, C), F32),
            pltpu.VMEM((T, 4, H, C), F32),
            pltpu.VMEM((T, 4, H, C), F32),
            pltpu.VMEM((T, 4, H, C), F32),
            pltpu.VMEM((8, C), jnp.int32),
            pltpu.SMEM((8, C), jnp.int32),
            pltpu.VMEM((2, NS, T, 16, C), BF),
            pltpu.VMEM((NS + 1, T, 16, C), BF),
            pltpu.VMEM((NS + 1, T, 16, C), BF),
            pltpu.VMEM((2, NS, T, 16, C), BF),
            pltpu.VMEM((2, NS, T, 16, C), BF),
            pltpu.VMEM((2, NS, T, C), F32),
            pltpu.VMEM((2, DIRS, T, C), F32),
            pltpu.VMEM((2, HALF, C), F32),
            pltpu.VMEM((HALF, C), BF),
            pltpu.VMEM((HALF, C), BF),
            pltpu.VMEM((HALF, C), BF),
            pltpu.VMEM((NP, CH, C), BF),
            pltpu.VMEM((CH, C), BF),
            pltpu.VMEM((NZ, CH, C), BF),
            pltpu.VMEM((CH, C), BF),
            pltpu.VMEM((HALF, C), BF),
            pltpu.VMEM((HALF, C), BF),
            dma((2 * T + 7,)),
            dma((2,)), dma((2,)), dma((2,)), dma((2,)),
            dma((2,)), dma((2, DIRS)),
            dma, dma, dma, dma, dma, dma, dma, dma, dma, dma,
        ],
        compiler_params=pltpu.CompilerParams(
            collective_id=0, has_side_effects=True, vmem_limit_bytes=44 * 2**20
        ),
        cost_estimate=pl.CostEstimate(
            flops=7247757312, bytes_accessed=10 * 2**20, transcendentals=2**20
        ),
        name="unet_conv_step",
    )(
        *(
            pltpu.with_memory_space_constraint(array, pltpu.HBM)
            for array in (
                hologram[0], weight, conv_bias[None], cotangent[0], tissue[0], owners,
                neighbours[0],
            )
        )
    )
    feat, ingrad, wgrad, bgrad = pl.pallas_call(
        finish,
        out_shape=(
            tiles,
            tiles,
            jax.ShapeDtypeStruct((9 * C, C), F32),
            jax.ShapeDtypeStruct((1, C), F32),
        ),
        in_specs=[vmem] * 3,
        out_specs=(hbm, hbm, hbm, vmem),
        scratch_shapes=[
            pltpu.VMEM((9 * C, C), F32), dma((3,))
        ],
        compiler_params=pltpu.CompilerParams(vmem_limit_bytes=10 * 2**20),
        name="hand_over",
    )(feat, ingrad, packed)
    return (
        feat[None], ingrad[None], wgrad.reshape(3, 3, C, C), bgrad.reshape(C)
    )


def solution(mesh):
    return jax.shard_map(
        local,
        mesh=mesh,
        in_specs=(
            P("replica", "space", None, None, None),
            P(),
            P(),
            P("replica", "space", None, None, None),
            P("replica", "space", None),
            P("replica", None),
            P("replica", None, None),
        ),
        out_specs=(
            P("replica", "space", None, None, None),
            P("replica", "space", None, None, None),
            P(),
            P(),
        ),
        check_vma=False,
    )
```

```python
import functools

import jax
import jax.numpy as jnp
from jax import lax
from jax.experimental import pallas as pl
from jax.experimental.pallas import tpu as pltpu
from jax.sharding import PartitionSpec as P

MESH = pl.DeviceIdType.MESH
BF = jnp.bfloat16
F32 = jnp.float32

NS = 16
NR = 16
NZ = 8
NP = 16
T = 2
H = 64
C = 128
PITCH = 80
WEST, FIRST, EAST = 7, 8, 72
CH = 48
OWNERS = 13
HALF = OWNERS * CH
FROM_ORIGIN_Z = (0, 1, 7, 2, 6, 3, 5, 4)
FROM_ORIGIN = sorted(
    range(16), key=lambda p: min(p // 4, 4 - p // 4) + min(p % 4, 4 - p % 4)
)
FAR_SPACE = sorted(
    ((dz, dy) for dz in range(8) for dy in range(2) if dz or dy),
    key=lambda d: -min(d[0], 8 - d[0]) - d[1],
)
FAR_PLANE = sorted(
    ((dx, dy) for dx in range(4) for dy in range(4) if dx or dy),
    key=lambda d: -min(d[0], 4 - d[0]) - min(d[1], 4 - d[1]),
)
CORNER_AT = (3, 0, 7, 4)
CORNER_ROW = (15, 0, 15, 0)
OFF = float(2**20)
PB = 16
DIRS = 4


def at80(row, off):
    return pl.multiple_of(row * PITCH, 8) + off


def kernel(
    holo, weight_in, bias_in, cot, tissue_in, owners_in, neigh_in,
    fv, iv, packed,
    weight, bias, tissue, owners, owners_s, neigh,
    hv, cv, gv, fh, fg, x3, w4, w4g, w9, w9g, pb, acc, bacc, raw2, drops,
    cotb, fb, gb, slots_v, slots_s,
    s1, r1a, r1b, s2, r2, s3, r3, arb, ah, arcv, half, brcv, csrc, crcv, dsrc, dall, erc,
    lsem, ss1, rs1, ss2, rs2, ss3, rs3, sa, ra, sb, rb, sc, rc, sd, rd, se, re,
):
    sp = lax.axis_index("space")
    rp = lax.axis_index("replica")
    z, ylo = lax.div(sp, 2), lax.rem(sp, 2)
    core = lax.rem(rp, 2)
    plane = lax.div(rp, 4) * 4 + lax.rem(lax.div(rp, 2), 2) * 2 + ylo

    def plane_dev(p):
        return (z * 2 + lax.rem(p, 2), lax.div(p, 2) * 2 + core)

    def z_dev(k):
        return (k * 2 + ylo, rp)

    partner = (sp, rp + 1 - 2 * core)
    r1 = (r1a, r1b)

    barrier = pltpu.get_barrier_semaphore()

    def near_space(d):
        return lax.rem(z + d[0], NZ) * 2 + lax.rem(ylo + d[1], 2)

    def near_plane(d):
        return lax.rem(lax.div(plane, 4) + d[0], 4) * 4 + lax.rem(lax.rem(plane, 4) + d[1], 4)

    for d in FAR_SPACE:
        pl.semaphore_signal(
            barrier, inc=1, device_id=(near_space(d), rp), device_id_type=MESH
        )
    for d in FAR_PLANE:
        pl.semaphore_signal(
            barrier, inc=1, device_id=plane_dev(near_plane(d)), device_id_type=MESH
        )
    pl.semaphore_signal(barrier, inc=1, device_id=partner, device_id_type=MESH)

    def load_h(t):
        return pltpu.make_async_copy(holo.at[t], hv.at[t], lsem.at[t])

    def load_c(t):
        return pltpu.make_async_copy(cot.at[t], cv.at[t], lsem.at[T + t])

    small = [
        pltpu.make_async_copy(src, dst, lsem.at[2 * T + 1 + i])
        for i, (src, dst) in enumerate(
            (
                (owners_in, owners), (owners_in, owners_s), (neigh_in, neigh),
                (tissue_in, tissue), (bias_in, bias), (weight_in, weight),
            )
        )
    ]
    for copy in small:
        copy.start()
    for t in range(T):
        load_h(t).start()
    for t in range(T):
        load_c(t).start()

    def copy1(ph, m, src):
        return pltpu.make_async_remote_copy(
            src_ref=s1.at[ph, m], dst_ref=r1[ph].at[src],
            send_sem=ss1.at[ph], recv_sem=rs1.at[ph],
            device_id=(m, rp), device_id_type=MESH,
        )

    def copy2(ph, j, src):
        return pltpu.make_async_remote_copy(
            src_ref=s2.at[ph, j], dst_ref=r2.at[ph, src],
            send_sem=ss2.at[ph], recv_sem=rs2.at[ph],
            device_id=(j, rp), device_id_type=MESH,
        )

    def copy3(ph, j, k):
        return pltpu.make_async_remote_copy(
            src_ref=s3.at[ph, j], dst_ref=r3.at[ph, k],
            send_sem=ss3.at[ph], recv_sem=rs3.at[ph, k],
            device_id=(j, rp), device_id_type=MESH,
        )

    def step(src_ref, dst_ref, send_sem, recv_sem):
        return pltpu.make_async_remote_copy(
            src_ref=src_ref, dst_ref=dst_ref, send_sem=send_sem, recv_sem=recv_sem,
            device_id=partner, device_id_type=MESH,
        )

    others = pl.ds(0, NS - 1)

    def step1(ph):
        return step(s1.at[ph, others], r1[ph].at[others], ss1.at[ph], rs1.at[ph])

    def step2(ph):
        return step(s2.at[ph, others], r2.at[ph, others], ss2.at[ph], rs2.at[ph])

    def far_space(fn):
        for d in FAR_SPACE:
            fn(near_space(d))

    def over_space(fn):
        def step(o, carry):
            fn(lax.rem(sp + o, NS))
            return carry

        lax.fori_loop(1, NS, step, 0)

    def exchange_out(ph, edges):
        for t in range(T):
            top, bottom, left, right = edges(t)
            for d, line in enumerate((bottom, top, right, left)):
                line = line.astype(BF)
                for q in range(4):
                    s1[ph, 4 * d + q, t] = line[16 * q : 16 * q + 16]
        r1[ph][sp] = s1[ph, sp]

    def exchange_send1(ph):
        far_space(lambda m: copy1(ph, m, sp).start())

    def exchange_route(ph):
        step1(ph).wait_recv()
        mine = lax.div(sp, 4)

        def route(j):
            for u in range(T):
                s = slots_s[mine, T * j + u]
                s2[ph, j, u] = r1[ph][lax.div(s, 2), lax.rem(s, 2)]

        def send(j):
            route(j)
            copy2(ph, j, sp).start()

        far_space(send)
        route(sp)
        r2[ph, sp] = s2[ph, sp]
        for k in range(DIRS):

            @pl.when(sp == CORNER_AT[k])
            def _():
                def corner(j):
                    for u in range(T):
                        s = slots_s[DIRS + k, T * j + u]
                        cells = r1[ph][lax.div(s, 2), lax.rem(s, 2)].astype(F32)
                        s3[ph, j, u : u + 1] = cells[CORNER_ROW[k] : CORNER_ROW[k] + 1]

                def give(j):
                    corner(j)
                    copy3(ph, j, k).start()

                over_space(give)
                corner(sp)
                r3[ph, k] = s3[ph, sp]

    def exchange_in(ph, frame):
        step2(ph).wait_recv()
        for t in range(T):
            for q in range(4):
                frame[t, pl.ds(FIRST + 16 * q, 16), :] = r2[ph, q, t].astype(F32)
                frame[t, pl.ds((H + 1) * PITCH + FIRST + 16 * q, 16), :] = r2[
                    ph, 4 + q, t
                ].astype(F32)
                for d, col in ((2, WEST), (3, EAST)):
                    frame[t, pl.ds((16 * q + 1) * PITCH + col, 16, stride=PITCH), :] = r2[
                        ph, 4 * d + q, t
                    ].astype(F32)
        for k in range(DIRS):

            @pl.when(sp != CORNER_AT[k])
            def _():
                copy3(ph, CORNER_AT[k], k).wait_recv()

        for t in range(T):
            for k, (row, col) in enumerate(
                ((0, WEST), (0, EAST), (H + 1, WEST), (H + 1, EAST))
            ):
                frame[t, pl.ds(row * PITCH + col, 1), :] = r3[ph, k, t : t + 1]

    def exchange_end(ph):
        step1(ph).wait_send()
        step2(ph).wait_send()
        for k in range(DIRS):

            @pl.when(sp == CORNER_AT[k])
            def _():
                step(
                    s3.at[ph, others], s3.at[ph, others], ss3.at[ph], rs3.at[ph, k]
                ).wait_send()

    def column(x):
        return pl.ds(PITCH + FIRST + x, H, stride=PITCH)

    for copy in small:
        copy.wait()

    own = jnp.broadcast_to(owners[...], (2 * DIRS, 2 * NS))
    near = jnp.full((2 * DIRS, 2 * NS), -1, jnp.int32)
    for tile in range(2 * NS):
        near = jnp.where(own == tile, neigh[:, tile : tile + 1], near)
    found = jnp.full((2 * DIRS, 2 * NS), 2 * NS, jnp.int32)
    for slot in range(2 * NS):
        found = jnp.where(near == owners_s[0, slot], slot, found)
    slots_v[:, 0 : 2 * NS] = found
    to_smem = pltpu.make_async_copy(slots_v, slots_s, lsem.at[2 * T])
    to_smem.start()

    zeros = jnp.zeros((C, C), BF)
    for r in range(4):
        for b in range(3):
            for q in range(2):
                a = r - q
                rows, cols = pl.ds((r * 3 + b) * C, C), pl.ds(q * C, C)
                if 0 <= a <= 2:
                    w4[rows, cols] = weight[a, b]
                else:
                    w4[rows, cols] = zeros
    line = lax.broadcasted_iota(jnp.int32, (C, 2 * C), 0)
    lane = lax.broadcasted_iota(jnp.int32, (C, 2 * C), 1)
    w4[12 * C : 13 * C, :] = jnp.where((line < H) == (lane < C), -OFF, 0.0).astype(BF)
    bacc[...] = jnp.zeros_like(bacc)
    for i in range(2):
        r1[i][NS] = jnp.zeros((T, 16, C), BF)
    for t in range(T):
        for p in range(H // 2):
            got = (1 - tissue[t : t + 1, p * C : (p + 1) * C]).astype(F32)
            raw2[t, 2 * p : 2 * p + 1, :] = got
            raw2[t, 2 * p + 1 : 2 * p + 2, :] = got
            drops[t, p : p + 1, :] = got
    prow = lax.broadcasted_iota(jnp.int32, (H // 2, C), 0)
    plane_lane = lax.broadcasted_iota(jnp.int32, (H // 2, C), 1)
    outer = (
        (plane_lane % H == 0)
        | (plane_lane % H == H - 1)
        | ((prow == 0) & (plane_lane < H))
        | ((prow == H // 2 - 1) & (plane_lane >= H))
    )
    for t in range(T):
        drops[t] = jnp.where(outer, 1.0, drops[t])
    for frame in (fh, fg):
        for t in range(T):
            frame[t, 0:PITCH, :] = jnp.zeros((PITCH, C), F32)
            frame[t, (H + 1) * PITCH : (H + 2) * PITCH, :] = jnp.zeros((PITCH, C), F32)
            frame[t, column(-1), :] = jnp.zeros((H, C), F32)
            frame[t, column(H), :] = jnp.zeros((H, C), F32)
    for t in range(T):
        load_h(t).wait()

        def fill(y, carry):
            fh[t, pl.ds(at80(y + 1, FIRST), H), :] = hv[t, y].astype(F32)
            return carry

        lax.fori_loop(0, H, fill, 0)
    exchange_out(
        0,
        lambda t: (
            hv[t, 0].astype(F32), hv[t, H - 1].astype(F32),
            fh[t, column(0), :], fh[t, column(H - 1), :],
        ),
    )
    pl.semaphore_wait(barrier, 2 * (NS - 1) + 1)
    exchange_send1(0)

    to_smem.wait()

    def shifts(dst, frame, t):
        def step(y, carry):
            for b in range(3):
                dst[t, y, :, b * C : (b + 1) * C] = frame[
                    t, pl.ds(at80(y, WEST + b), H), :
                ].astype(BF)
            return carry

        lax.fori_loop(0, H + 2, step, 0, unroll=2)

    nb = (H // 2) // PB
    bias2 = jnp.concatenate([bias[...], bias[...]], axis=1)
    sub = lax.broadcasted_iota(jnp.int32, (H, C), 0)
    lanes = lax.broadcasted_iota(jnp.int32, (H, C), 1)
    eye = sub == lanes % H

    def window(src, t, p):
        return jnp.concatenate([src[t, 2 * p + r] for r in range(4)], axis=1)

    def activate(pre):
        sigma = 0.5 * jnp.tanh(0.5 * pre) + 0.5
        act = pre * sigma
        return act, sigma + act * (1.0 - sigma)

    def forward(t):
        def step(i, carry):
            p0 = i * PB
            parts = []
            for k in range(PB):
                drop = jnp.where(eye, drops[t, pl.ds(p0 + k, 1), :], 0.0).astype(BF)
                parts.append(jnp.concatenate([window(x3, t, p0 + k), drop], axis=1))
            pre = jnp.dot(
                jnp.concatenate(parts, axis=0), w4[...], preferred_element_type=F32
            ) + bias2
            act, slope = activate(pre)
            total = jnp.zeros((8, C), F32)
            for k in range(PB):
                for q in range(2):
                    y = 2 * (p0 + k) + q
                    rows, cols = slice(k * H, (k + 1) * H), slice(q * C, (q + 1) * C)
                    fv[t, y] = act[rows, cols].astype(BF)
                    wide = cv[t, y].astype(F32)
                    cotb[t, 2, pl.ds(y, 1), :] = wide[:1]
                    cotb[t, 3, pl.ds(y, 1), :] = wide[H - 1 :]
                    g = (wide * slope[rows, cols]).astype(BF)
                    gv[t, y] = g
                    wide = g.astype(F32)
                    fg[t, pl.ds(at80(y + 1, FIRST), H), :] = wide
                    total = total + jnp.sum(wide.reshape(H // 8, 8, C), axis=0)
            bacc[...] += total
            return carry

        lax.fori_loop(0, nb, step, 0, unroll=True)

    def weights(t):
        left = jnp.concatenate(
            [
                jnp.concatenate([gv[t, 2 * p + q] for p in range(H // 2)], axis=0).T
                for q in range(2)
            ],
            axis=0,
        )
        right = jnp.concatenate([window(x3, t, p) for p in range(H // 2)], axis=0)
        got = jnp.dot(left, right, preferred_element_type=F32)
        acc[...] = got if t == 0 else acc[...] + got

    def backward(t):
        def step(i, carry):
            p0 = i * PB
            got = jnp.dot(
                jnp.concatenate([window(x3, t, p0 + k) for k in range(PB)], axis=0),
                w4g[...],
                preferred_element_type=F32,
            )
            for k in range(PB):
                for q in range(2):
                    iv[t, 2 * (p0 + k) + q] = got[
                        k * H : (k + 1) * H, q * C : (q + 1) * C
                    ].astype(BF)
            return carry

        lax.fori_loop(0, nb, step, 0)

    def patches(frame):
        for t in range(T):
            for side in range(4):
                rows = slice((t * 4 + side) * H, (t * 4 + side + 1) * H)
                y0 = H - 1 if side == 1 else 0
                x0 = H - 1 if side == 3 else 0
                stride = PITCH if side >= 2 else None
                for a in range(3):
                    for b in range(3):
                        got = frame[t, pl.ds((y0 + a) * PITCH + WEST + x0 + b, H, stride=stride), :]
                        tap = a * 3 + b
                        pb[rows, tap * C : (tap + 1) * C] = got.astype(BF)

    def put_columns(dst, src, t):
        low = lax.broadcasted_iota(jnp.int32, (16, C), 0) == 0
        high = lax.broadcasted_iota(jnp.int32, (16, C), 0) == 15

        def step(y, carry):
            first = dst[t, y, 0:16, :].astype(F32)
            dst[t, y, 0:16, :] = jnp.where(low, src[t, 2, pl.ds(y, 1), :], first).astype(BF)
            last = dst[t, y, H - 16 : H, :].astype(F32)
            dst[t, y, H - 16 : H, :] = jnp.where(
                high, src[t, 3, pl.ds(y, 1), :], last
            ).astype(BF)
            return carry

        lax.fori_loop(0, H, step, 0, unroll=4)

    def put_rows(dst, src, t):
        dst[t, 0] = src[t, 0].astype(BF)
        dst[t, H - 1] = src[t, 1].astype(BF)

    copy_a = pltpu.make_async_remote_copy(
        src_ref=ah, dst_ref=arcv, send_sem=sa, recv_sem=ra,
        device_id=partner, device_id_type=MESH,
    )

    def chunk(p):
        return pl.ds(pl.multiple_of(p * CH, 16), CH)

    def copy_b(p, src):
        return pltpu.make_async_remote_copy(
            src_ref=half.at[chunk(p)], dst_ref=brcv.at[src],
            send_sem=sb, recv_sem=rb,
            device_id=plane_dev(p), device_id_type=MESH,
        )

    def copy_c(k, src):
        return pltpu.make_async_remote_copy(
            src_ref=csrc, dst_ref=crcv.at[src], send_sem=sc, recv_sem=rc,
            device_id=z_dev(k), device_id_type=MESH,
        )

    def copy_d(p, src):
        return pltpu.make_async_remote_copy(
            src_ref=dsrc, dst_ref=dall.at[chunk(src)], send_sem=sd, recv_sem=rd,
            device_id=plane_dev(p), device_id_type=MESH,
        )

    copy_e = pltpu.make_async_remote_copy(
        src_ref=dall, dst_ref=erc, send_sem=se, recv_sem=re,
        device_id=partner, device_id_type=MESH,
    )

    in_plane, in_ring = pl.ds(0, NP - 1), pl.ds(0, NZ - 1)

    def step_b(rows):
        return step(half.at[pl.ds(0, rows)], brcv.at[in_plane], sb, rb)

    def step_c():
        return step(crcv.at[in_ring], crcv.at[in_ring], sc, rc)

    def step_d(rows):
        return step(brcv.at[in_plane], dall.at[pl.ds(0, rows)], sd, rd)

    owner = plane < OWNERS

    def stage_a():
        ah[...] = arb[1 - core].astype(BF)
        copy_a.start()

    def stage_b():
        copy_a.wait_recv()
        half[...] = (arb[core] + arcv[...].astype(F32)).astype(BF)
        for d in FAR_PLANE:
            p = near_plane(d)
            pl.when(p < OWNERS)(lambda p=p: copy_b(p, plane).start())

        @pl.when(owner)
        def _():
            brcv[plane] = half[chunk(plane)]

    def stage_c():
        @pl.when(owner)
        def _():
            step_b(HALF).wait_recv()
            total = brcv[0].astype(F32)
            for p in range(1, NP):
                total = total + brcv[p].astype(F32)
            csrc[...] = total.astype(BF)
            for k in FROM_ORIGIN_Z:
                pl.when(z != k)(lambda k=k: copy_c(k, z).start())
            crcv[z] = csrc[...]

    def stage_d():
        @pl.when(owner)
        def _():
            step_c().wait_recv()
            total = crcv[0].astype(F32)
            for k in range(1, NZ):
                total = total + crcv[k].astype(F32)
            dsrc[...] = (total * float(NS * NR * T * H * H) ** -0.5).astype(BF)
            for p in FROM_ORIGIN:
                pl.when(plane != p)(lambda p=p: copy_d(p, plane).start())
            dall[chunk(plane)] = dsrc[...]

    def stage_e():
        @pl.when(owner)
        def _():
            step_d(HALF - CH).wait_recv()

        @pl.when(jnp.logical_not(owner))
        def _():
            step_d(HALF).wait_recv()

        copy_e.start()

    def put_gradient(tap, block, add):
        def put(i, lo, size, val):
            rows = slice(lo, lo + size)
            arb[i, rows] = arb[i, rows] + val if add else val

        if tap < 4:
            put(0, tap * C, C, block)
        elif tap == 4:
            put(0, 4 * C, H, block[:H])
            put(1, 0, H, block[H:])
        else:
            put(1, H + (tap - 5) * C, C, block)

    shifts(x3, fh, 0)
    for t in range(T):
        load_c(t).wait()
    shifts(x3, fh, 1)
    for tap in range(9):
        a, b = tap // 3, tap % 3
        w9[tap * C : (tap + 1) * C, :] = weight[a, b]
    w9[9 * C : 10 * C, :] = jnp.full((C, C), -OFF, BF)
    for t in range(T):
        cotb[t, 0] = cv[t, 0].astype(F32)
        cotb[t, 1] = cv[t, H - 1].astype(F32)
        for side, keep in enumerate(
            (
                jnp.where(lanes == sub, raw2[t, 0:1, :], 0.0),
                jnp.where(lanes == sub + H, raw2[t, H - 1 : H, :], 0.0),
                jnp.where(lanes == sub % 2 * H, raw2[t], 0.0),
                jnp.where(lanes == sub % 2 * H + H - 1, raw2[t], 0.0),
            )
        ):
            rows = slice((t * 4 + side) * H, (t * 4 + side + 1) * H)
            pb[rows, 9 * C : 10 * C] = keep.astype(BF)

    forward(0)
    exchange_route(0)
    forward(1)
    weights(0)
    weights(1)
    for tap in range(9):
        a, b = tap // 3, tap % 3
        lo = slice((a * 3 + b) * C, (a * 3 + b + 1) * C)
        hi = slice(((a + 1) * 3 + b) * C, ((a + 1) * 3 + b + 1) * C)
        put_gradient(tap, acc[0:C, lo] + acc[C : 2 * C, hi], False)

    exchange_in(0, fh)
    patches(fh)
    pre = jnp.dot(pb[...], w9[...], preferred_element_type=F32) + bias[...]
    act, slope = activate(pre)
    fb[...] = act.reshape(T, 4, H, C)
    grads = (cotb[...].reshape(T * 4 * H, C) * slope).astype(BF).astype(F32)
    gb[...] = grads.reshape(T, 4, H, C)
    spot = lax.broadcasted_iota(jnp.int32, (T * 4 * H, C), 0)
    once = (spot % (4 * H) < 2 * H) | ((spot % H > 0) & (spot % H < H - 1))
    grads = jnp.where(once, grads, 0.0)
    outer_w = jnp.dot(
        grads.T.astype(BF), pb[:, 0 : 9 * C], preferred_element_type=F32
    )
    for tap in range(9):
        put_gradient(tap, outer_w[:, tap * C : (tap + 1) * C], True)
    bsum = jnp.sum(bacc[...], axis=0, keepdims=True) + jnp.sum(grads, axis=0, keepdims=True)
    first = lax.broadcasted_iota(jnp.int32, (HALF - 576, C), 0) == 0
    arb[0, 576:HALF] = jnp.where(first, bsum, 0.0)
    arb[1, 576:HALF] = jnp.zeros((HALF - 576, C), F32)
    stage_a()

    exchange_out(1, lambda t: tuple(gb[t, side] for side in range(4)))
    exchange_send1(1)
    stage_b()

    for t in range(T):
        put_rows(fv, fb, t)
        put_columns(fv, fb, t)
        fg[t, pl.ds(PITCH + FIRST, H), :] = gb[t, 0]
        fg[t, pl.ds(H * PITCH + FIRST, H), :] = gb[t, 1]
        fg[t, column(0), :] = gb[t, 2]
        fg[t, column(H - 1), :] = gb[t, 3]
    for r in range(4):
        for b in range(3):
            for q in range(2):
                a = r - q
                rows, cols = pl.ds((r * 3 + b) * C, C), pl.ds(q * C, C)
                if 0 <= a <= 2:
                    turned = weight[2 - a, 2 - b].astype(F32).T.astype(BF)
                    w4g[rows, cols] = turned
                    if q == 0:
                        w9g[(a * 3 + b) * C : (a * 3 + b + 1) * C, :] = turned
                else:
                    w4g[rows, cols] = zeros
    shifts(x3, fg, 0)
    shifts(x3, fg, 1)
    exchange_route(1)
    stage_c()
    backward(0)
    backward(1)
    stage_d()

    exchange_in(1, fg)
    patches(fg)
    got = jnp.dot(pb[:, 0 : 9 * C], w9g[...], preferred_element_type=F32)
    fb[...] = got.reshape(T, 4, H, C)
    for t in range(T):
        put_rows(iv, fb, t)
        put_columns(iv, fb, t)
    exchange_end(0)
    exchange_end(1)
    copy_a.wait_send()

    @pl.when(owner)
    def _():
        step_b(HALF - CH).wait_send()
        step_c().wait_send()

    @pl.when(jnp.logical_not(owner))
    def _():
        step_b(HALF).wait_send()

    stage_e()

    @pl.when(owner)
    def _():
        step_d(HALF).wait_send()

    packed[core] = dall[...]
    copy_e.wait()
    packed[1 - core] = erc[...]


def finish(feat, ingrad, packed, feat_out, ingrad_out, wgrad_out, bgrad, wgrad, sem):
    copies = [
        pltpu.make_async_copy(feat, feat_out, sem.at[0]),
        pltpu.make_async_copy(ingrad, ingrad_out, sem.at[1]),
        pltpu.make_async_copy(wgrad, wgrad_out, sem.at[2]),
    ]
    for copy in copies[:2]:
        copy.start()
    for tap in range(9):
        if tap < 4:
            block = packed[0, tap * C : (tap + 1) * C]
        elif tap == 4:
            block = jnp.concatenate([packed[0, 4 * C : 4 * C + H], packed[1, 0:H]], axis=0)
        else:
            block = packed[1, H + (tap - 5) * C : H + (tap - 4) * C]
        wgrad[tap * C : (tap + 1) * C, :] = block.astype(F32).T
    copies[2].start()
    bgrad[...] = packed[0, 576 : 576 + 16].astype(F32)[0:1]
    for copy in copies:
        copy.wait()


def local(hologram, weight, conv_bias, cotangent, tissue, owners, neighbours):
    vmem = pl.BlockSpec(memory_space=pltpu.VMEM)
    hbm = pl.BlockSpec(memory_space=pltpu.HBM)
    tiles = jax.ShapeDtypeStruct((T, H, H, C), BF)
    dma = pltpu.SemaphoreType.DMA
    feat, ingrad, packed = pl.pallas_call(
        kernel,
        out_shape=(
            pltpu.VMEM((T, H, H, C), BF),
            pltpu.VMEM((T, H, H, C), BF),
            pltpu.VMEM((2, HALF, C), BF),
        ),
        in_specs=[hbm] * 7,
        out_specs=(vmem, vmem, vmem),
        scratch_shapes=[
            pltpu.VMEM((3, 3, C, C), BF),
            pltpu.VMEM((1, C), F32),
            pltpu.VMEM((T, H * H), jnp.int32),
            pltpu.VMEM((1, 2 * NS), jnp.int32),
            pltpu.SMEM((1, 2 * NS), jnp.int32),
            pltpu.VMEM((2 * DIRS, 2 * NS), jnp.int32),
            pltpu.VMEM((T, H, H, C), BF),
            pltpu.VMEM((T, H, H, C), BF),
            pltpu.VMEM((T, H, H, C), BF),
            pltpu.VMEM((T, (H + 3) * PITCH, C), F32),
            pltpu.VMEM((T, (H + 3) * PITCH, C), F32),
            pltpu.VMEM((T, H + 2, H, 3 * C), BF),
            pltpu.VMEM((13 * C, 2 * C), BF),
            pltpu.VMEM((12 * C, 2 * C), BF),
            pltpu.VMEM((10 * C, C), BF),
            pltpu.VMEM((9 * C, C), BF),
            pltpu.VMEM((T * 4 * H, 10 * C), BF),
            pltpu.VMEM((2 * C, 12 * C), F32),
            pltpu.VMEM((8, C), F32),
            pltpu.VMEM((T, H, C), F32),
            pltpu.VMEM((T, H // 2, C), F32),
            pltpu.VMEM((T, 4, H, C), F32),
            pltpu.VMEM((T, 4, H, C), F32),
            pltpu.VMEM((T, 4, H, C), F32),
            pltpu.VMEM((8, C), jnp.int32),
            pltpu.SMEM((8, C), jnp.int32),
            pltpu.VMEM((2, NS, T, 16, C), BF),
            pltpu.VMEM((NS + 1, T, 16, C), BF),
            pltpu.VMEM((NS + 1, T, 16, C), BF),
            pltpu.VMEM((2, NS, T, 16, C), BF),
            pltpu.VMEM((2, NS, T, 16, C), BF),
            pltpu.VMEM((2, NS, T, C), F32),
            pltpu.VMEM((2, DIRS, T, C), F32),
            pltpu.VMEM((2, HALF, C), F32),
            pltpu.VMEM((HALF, C), BF),
            pltpu.VMEM((HALF, C), BF),
            pltpu.VMEM((HALF, C), BF),
            pltpu.VMEM((NP, CH, C), BF),
            pltpu.VMEM((CH, C), BF),
            pltpu.VMEM((NZ, CH, C), BF),
            pltpu.VMEM((CH, C), BF),
            pltpu.VMEM((HALF, C), BF),
            pltpu.VMEM((HALF, C), BF),
            dma((2 * T + 7,)),
            dma((2,)), dma((2,)), dma((2,)), dma((2,)),
            dma((2,)), dma((2, DIRS)),
            dma, dma, dma, dma, dma, dma, dma, dma, dma, dma,
        ],
        compiler_params=pltpu.CompilerParams(
            collective_id=0, has_side_effects=True, vmem_limit_bytes=44 * 2**20
        ),
        cost_estimate=pl.CostEstimate(
            flops=7247757312, bytes_accessed=10 * 2**20, transcendentals=2**20
        ),
        name="unet_conv_step",
    )(
        *(
            pltpu.with_memory_space_constraint(array, pltpu.HBM)
            for array in (
                hologram[0], weight, conv_bias[None], cotangent[0], tissue[0], owners,
                neighbours[0],
            )
        )
    )
    feat, ingrad, wgrad, bgrad = pl.pallas_call(
        finish,
        out_shape=(
            tiles,
            tiles,
            jax.ShapeDtypeStruct((9 * C, C), F32),
            jax.ShapeDtypeStruct((1, C), F32),
        ),
        in_specs=[vmem] * 3,
        out_specs=(hbm, hbm, hbm, vmem),
        scratch_shapes=[
            pltpu.VMEM((9 * C, C), F32), dma((3,))
        ],
        compiler_params=pltpu.CompilerParams(vmem_limit_bytes=10 * 2**20),
        name="hand_over",
    )(feat, ingrad, packed)
    return (
        feat[None], ingrad[None], wgrad.reshape(3, 3, C, C), bgrad.reshape(C)
    )


def solution(mesh):
    return jax.shard_map(
        local,
        mesh=mesh,
        in_specs=(
            P("replica", "space", None, None, None),
            P(),
            P(),
            P("replica", "space", None, None, None),
            P("replica", "space", None),
            P("replica", None),
            P("replica", None, None),
        ),
        out_specs=(
            P("replica", "space", None, None, None),
            P("replica", "space", None, None, None),
            P(),
            P(),
        ),
        check_vma=False,
    )
```
